256 devices in a mesh: uly: 4 (over x_lo, core), blk: 64 (over x_hi, y, z).
Axes of the slice: x: 4 (x_hi: 2, x_lo: 2; x = x_hi * 2 + x_lo), y: 4, z: 8, core: 2. Of those that a mesh axis runs over, the one named last changes fastest.
Arguments:
- image_tokens: bfloat16 [12288, 1536], P(('uly', 'blk')), may hold values from -11 to 11
- text_tokens: bfloat16 [333, 1536], replicated, may hold values from -6 to 6
- w_query_key: bfloat16 [1536, 2, 1536], P(None, None, 'uly'), may hold values from -0.21875 to 0.21875
- w_value: bfloat16 [1536, 1536], P(None, 'uly'), may hold values from -0.4375 to 0.4375
- qkv_bias: float32 [3, 1536], P(None, 'uly'), may hold values from -3 to 3
- w_text: bfloat16 [1536, 2, 1536], P(None, None, 'uly'), may hold values from -0.21875 to 0.21875
- text_bias: float32 [2, 1536], P(None, 'uly'), may hold values from -3 to 3
- w_out: bfloat16 [1536, 1536], P('uly'), may hold values from -0.15625 to 0.15625
- out_bias: float32 [1536], replicated, may hold values from -3 to 3
Outputs:
- attn_out: bfloat16 [12288, 1536], P(('uly', 'blk'))
The draws below stay inside these ranges and needn't reach their ends.
All inputs are finite; a program needn't handle non-finite values.
Results may differ from the reference program's by a relative error of at most 0.017.
The reference program's roundings to bfloat16 on the way count: a program that leaves them out, or rounds other values in their place, can miss the bound.
Values may be sent and summed in bfloat16 or wider, within the bound.
No kernel may reach another device: no remote copies, remote signals or barrier semaphores. Data moves between devices by JAX's collectives and lax.ppermute only.
A program may use at most 128 MiB of HBM per device.

```python
import math
import jax
import jax.numpy as jnp
from jax import lax

D = 1536
HEADS = 24
HEAD_DIM = 64
TEXT = 333
TOKENS = 12288


def draw_image_tokens(key, part):
    key = jax.random.fold_in(key, 11)
    entries = jnp.clip(jax.random.normal(key, (TOKENS, D), jnp.float32), -6.0, 6.0)
    return entries.astype(jnp.bfloat16)


def shard_levels(rng, dims, cuts, low, high):
    level = 1.0
    for axis_at, blocks in cuts:
        heights = jax.random.uniform(jax.random.fold_in(jax.random.fold_in(rng, 6), axis_at), (blocks,), jnp.float32, low / len(cuts), high / len(cuts))
        level = level * jnp.repeat(jnp.exp(heights), dims[axis_at] // blocks).reshape((-1,) + (1,) * (len(dims) - 1 - axis_at))
    return level


def noise(rng, dims, spread, bound, cuts=(), kind=jnp.bfloat16):
    loudness = shard_levels(rng, dims, cuts, -0.22, 0.18) if cuts else 1.0
    values = jax.random.normal(rng, dims, jnp.float32) * spread * loudness
    return jnp.minimum(jnp.maximum(values, -bound), bound).astype(kind)


def setup_inputs(seed: int = 0) -> dict:
    streams_of = jax.random.split(jax.random.key(seed), 10)
    return {
        "image_tokens": draw_image_tokens(jax.random.fold_in(streams_of[9], 71), 0),
        "text_tokens": noise(streams_of[1], (TEXT, D), 1.0, 6.0),
        "w_query_key": noise(streams_of[2], (D, 2, D), (D * 4 // 9) ** -0.5, 0.21875, ((2, 4),)),
        "w_value": noise(streams_of[3], (D, D), (D // 9) ** -0.5, 0.4375, ((1, 4),)),
        "qkv_bias": noise(streams_of[4], (3, D), 0.5, 3.0, ((1, 4),), jnp.float32),
        "w_text": noise(streams_of[5], (D, 2, D), (D * 4 // 9) ** -0.5, 0.21875, ((2, 4),)),
        "text_bias": noise(streams_of[6], (2, D), 0.5, 3.0, ((1, 4),), jnp.float32),
        "w_out": noise(streams_of[7], (D, D), D ** -0.5, 0.15625, ((0, 4),)),
        "out_bias": noise(streams_of[8], (D,), 0.5, 3.0, (), jnp.float32),
    }


def head_attention(query_head, key_head, value_head):
    scores = jnp.dot(query_head, key_head.T, preferred_element_type=jnp.float32) * (HEAD_DIM ** -0.5)
    row_top = jnp.max(scores, axis=1, keepdims=True)
    exp_scores = jnp.exp(scores - row_top)
    row_total = jnp.sum(exp_scores, axis=1, keepdims=True)
    mixed_rows = jnp.dot(exp_scores.astype(jnp.bfloat16), value_head, preferred_element_type=jnp.float32)
    return (mixed_rows / row_total).astype(jnp.bfloat16)


def reference(image_tokens, text_tokens, w_query_key, w_value, qkv_bias, w_text, text_bias, w_out, out_bias):
    queries = (jnp.dot(image_tokens, w_query_key[:, 0, :], preferred_element_type=jnp.float32) + qkv_bias[0]).astype(jnp.bfloat16)
    keys_image = (jnp.dot(image_tokens, w_query_key[:, 1, :], preferred_element_type=jnp.float32) + qkv_bias[1]).astype(jnp.bfloat16)
    values = (jnp.dot(image_tokens, w_value, preferred_element_type=jnp.float32) + qkv_bias[2]).astype(jnp.bfloat16)
    text_keys = (jnp.dot(text_tokens, w_text[:, 0, :], preferred_element_type=jnp.float32) + text_bias[0]).astype(jnp.bfloat16)
    text_values = (jnp.dot(text_tokens, w_text[:, 1, :], preferred_element_type=jnp.float32) + text_bias[1]).astype(jnp.bfloat16)
    all_keys = jnp.concatenate([text_keys, keys_image], axis=0)
    all_values = jnp.concatenate([text_values, values], axis=0)
    key_heads = all_keys.reshape(TEXT + TOKENS, HEADS, HEAD_DIM).transpose(1, 0, 2)
    value_heads = all_values.reshape(TEXT + TOKENS, HEADS, HEAD_DIM).transpose(1, 0, 2)
    block_rows = math.gcd(TOKENS, 512)
    query_blocks = queries.reshape(TOKENS // block_rows, block_rows, HEADS, HEAD_DIM)

    def one_head(operands):
        return head_attention(operands[0], operands[1], operands[2])

    def one_block(query_block):
        return lax.map(one_head, (query_block.transpose(1, 0, 2), key_heads, value_heads))

    attended = lax.map(one_block, query_blocks)
    attention = attended.transpose(0, 2, 1, 3).reshape(TOKENS, D)
    return (jnp.dot(attention, w_out, preferred_element_type=jnp.float32) + out_bias).astype(jnp.bfloat16)
```

```python
import functools

import jax
import jax.numpy as jnp
from jax import lax
from jax.experimental import pallas as pl
from jax.experimental.pallas import tpu as pltpu
from jax.sharding import PartitionSpec as P

HEAD_DIM = 64
AXES = ("uly", "blk")
X, CORE, Y, Z = 4, 2, 4, 8
ONES = 16
STATS = 32
LOG2_SCALE = 1.4426950408889634 * HEAD_DIM**-0.5
SAFE_SQUARE = 3600.0
MASKED = -1e30
BF16, F32 = jnp.bfloat16, jnp.float32


def device_id(x, core, y, z):
    return ((x % 2) * CORE + core) * (2 * Y * Z) + (x // 2) * (Y * Z) + y * Z + z


def places():
    return [
        (x, core, y, z) for x in range(X) for core in range(CORE) for y in range(Y) for z in range(Z)
    ]


def fetch(array, dx=0, dcore=0, dy=0, dz=0):
    pairs = [
        (
            device_id((x + dx) % X, (core + dcore) % CORE, (y + dy) % Y, (z + dz) % Z),
            device_id(x, core, y, z),
        )
        for x, core, y, z in places()
    ]
    return lax.ppermute(array, AXES, pairs)


def call(kernel, out_shape, flops, *operands, exps=0, aliases=None, name=None):
    spec = pl.BlockSpec(memory_space=pltpu.VMEM)
    moved = sum(a.size * a.dtype.itemsize for a in operands)
    return pl.pallas_call(
        kernel,
        out_shape=out_shape,
        in_specs=[spec] * len(operands),
        out_specs=jax.tree.map(lambda _: spec, out_shape),
        input_output_aliases=aliases or {},
        compiler_params=pltpu.CompilerParams(vmem_limit_bytes=40 << 20),
        cost_estimate=pl.CostEstimate(flops=flops, bytes_accessed=moved, transcendentals=exps),
        name=name,
    )(*operands)


def shape(dims, dtype):
    return jax.ShapeDtypeStruct(dims, dtype)


def project_kernel(own_ref, other_ref, w_ref, bias_ref, q_ref, kv_ref):
    heads = q_ref.shape[0]
    width = heads * HEAD_DIM
    half = own_ref.shape[0]
    for at, x_ref in enumerate((own_ref, other_ref)):
        rows = jnp.dot(x_ref[...], w_ref[...], preferred_element_type=F32) + bias_ref[0:1, :]
        columns = rows.T.astype(BF16)
        here = slice(at * half, (at + 1) * half)
        for h in range(heads):
            cut = h * HEAD_DIM
            q_ref[h, :, here] = columns[cut : cut + HEAD_DIM]
            kv_ref[h, :HEAD_DIM, here] = columns[width + cut : width + cut + HEAD_DIM]
            kv_ref[h, HEAD_DIM:, here] = columns[2 * width + cut : 2 * width + cut + HEAD_DIM]


def text_kernel(count, text_ref, w_ref, bias_ref, kv_ref):
    heads = kv_ref.shape[0]
    width = heads * HEAD_DIM
    rows = jnp.dot(text_ref[...], w_ref[...], preferred_element_type=F32) + bias_ref[0:1, :]
    columns = rows.T
    inside = lax.broadcasted_iota(jnp.int32, columns.shape, 1) < count
    columns = jnp.where(inside, columns, 0.0).astype(BF16)
    for h in range(heads):
        cut = h * HEAD_DIM
        kv_ref[h, :HEAD_DIM, :] = columns[cut : cut + HEAD_DIM]
        kv_ref[h, HEAD_DIM:, :] = columns[width + cut : width + cut + HEAD_DIM]


def scale_queries(parts, q2_ref, norm_ref):
    for h in range(q2_ref.shape[0]):
        largest = None
        for at, part in enumerate(parts):
            scaled = part[h].astype(F32) * LOG2_SCALE
            high = scaled.astype(BF16)
            low = (scaled - high.astype(F32)).astype(BF16)
            here = slice(at * part.shape[2], (at + 1) * part.shape[2])
            q2_ref[h, :HEAD_DIM, here] = high
            q2_ref[h, HEAD_DIM:, here] = low
            top = jnp.max(jnp.sum(scaled * scaled, axis=0, keepdims=True), axis=1, keepdims=True)
            largest = top if largest is None else jnp.maximum(largest, top)
        norm_ref[h] = jnp.broadcast_to(largest, norm_ref.shape[1:])


def keys_of(parts, h):
    return jnp.concatenate([k[h, :HEAD_DIM, :] for k, _ in parts], axis=1)


def values_of(parts, h, count):
    values = jnp.concatenate([v[h, -HEAD_DIM:, :] for _, v in parts], axis=1)
    ones = jnp.ones((ONES, values.shape[1]), BF16)
    if count is not None:
        inside = lax.broadcasted_iota(jnp.int32, ones.shape, 1) < count
        ones = jnp.where(inside, 1.0, 0.0).astype(BF16)
    return jnp.concatenate([values, ones], axis=0)


def attend(parts, q2_ref, norm_ref, bound, state_in, acc_ref, m_ref, bound_ref, tile, count=None):
    heads, _, queries = q2_ref.shape
    worst = None
    for h in range(heads):
        keys = keys_of(parts, h).astype(F32)
        top = jnp.max(jnp.sum(keys * keys, axis=0, keepdims=True), axis=1, keepdims=True)
        product = top * norm_ref[h, 0:1, 0:1]
        worst = product if worst is None else jnp.maximum(worst, product)
    if bound is not None:
        worst = jnp.maximum(worst, bound[0:1, 0:1])
    bound_ref[...] = jnp.broadcast_to(worst, bound_ref.shape)
    safe = jnp.max(worst) <= SAFE_SQUARE

    def doubled_keys(h):
        keys = keys_of(parts, h)
        return jnp.concatenate([keys, keys], axis=0).T

    @pl.when(safe)
    def _():
        for h in range(heads):
            keys, values = doubled_keys(h), values_of(parts, h, count)
            for at in range(0, queries, tile):
                here = slice(at, at + tile)
                scores = jnp.dot(keys, q2_ref[h, :, here], preferred_element_type=F32)
                weights = jnp.exp2(scores).astype(BF16)
                term = jnp.dot(values, weights, preferred_element_type=F32)
                acc_ref[h, :, here] = term if state_in is None else state_in[0][h, :, here] + term
        m_ref[...] = jnp.zeros_like(m_ref) if state_in is None else state_in[1][...]

    @pl.when(jnp.logical_not(safe))
    def _():
        step = 128

        def one_head(h, carry):
            keys, values = doubled_keys(h), values_of(parts, h, count)

            def one_tile(at, carry):
                here = pl.ds(pl.multiple_of(at * step, step), step)
                scores = jnp.dot(keys, q2_ref[h, :, here], preferred_element_type=F32)
                if count is not None:
                    inside = lax.broadcasted_iota(jnp.int32, scores.shape, 0) < count
                    scores = jnp.where(inside, scores, MASKED)
                top = jnp.max(scores, axis=0, keepdims=True)
                if state_in is not None:
                    before = state_in[1][h, 0:1, here]
                    top = jnp.maximum(top, before)
                weights = jnp.exp2(scores - top).astype(BF16)
                term = jnp.dot(values, weights, preferred_element_type=F32)
                if state_in is not None:
                    term = term + state_in[0][h, :, here] * jnp.exp2(before - top)
                acc_ref[h, :, here] = term
                m_ref[h, :, here] = jnp.broadcast_to(top, (m_ref.shape[1], step))
                return carry

            return lax.fori_loop(0, queries // step, one_tile, carry)

        lax.fori_loop(0, heads, one_head, 0)


def text_attend_kernel(count, q_ref, kv_ref, acc_ref, m_ref, q2_ref, norm_ref, bound_ref):
    scale_queries([q_ref], q2_ref, norm_ref)
    parts = [(kv_ref, kv_ref)]
    tile = q2_ref.shape[2]
    attend(parts, q2_ref, norm_ref, None, None, acc_ref, m_ref, bound_ref, tile, count)


def first_kernel(n_parts, tile, *refs):
    q_refs, kv_refs = refs[:Y], refs[Y : Y + n_parts]
    acc_ref, m_ref, bound_ref, q2_ref, norm_ref = refs[Y + n_parts :]
    scale_queries(q_refs, q2_ref, norm_ref)
    parts = [(r, r) for r in kv_refs]
    attend(parts, q2_ref, norm_ref, None, None, acc_ref, m_ref, bound_ref, tile)


def next_kernel(n_parts, tile, *refs):
    kv_refs = refs[:n_parts]
    q2_ref, norm_ref, acc_in, m_in, bound_in, acc_ref, m_ref, bound_ref = refs[n_parts:]
    parts = [(r, r) for r in kv_refs]
    attend(parts, q2_ref, norm_ref, bound_in, (acc_in, m_in), acc_ref, m_ref, bound_ref, tile)


def three_parts(value):
    high = value.astype(BF16).astype(F32)
    middle = (value - high).astype(BF16).astype(F32)
    return [high, middle, value - high - middle]


def last_kernel(tile, k_ref, v_ref, *refs):
    q2_ref, norm_ref, acc_in, m_in, bound_in, acc_ref, m_ref, bound_ref = refs[:8]
    packs = refs[8:]
    parts = [(k_ref, v_ref)]
    attend(parts, q2_ref, norm_ref, bound_in, (acc_in, m_in), acc_ref, m_ref, bound_ref, tile)
    heads, _, queries = q2_ref.shape
    mine = queries // Y
    for at, pack in enumerate(packs):
        here = slice((at + 1) * mine, (at + 2) * mine)
        rows = []
        for h in range(heads):
            pack[h * HEAD_DIM : (h + 1) * HEAD_DIM, :] = acc_ref[h, :HEAD_DIM, here].astype(BF16)
            rows += three_parts(acc_ref[h, HEAD_DIM : HEAD_DIM + 1, here])
            rows += three_parts(m_ref[h, 0:1, here])
        rows.append(jnp.zeros((STATS - len(rows), mine), F32))
        pack[heads * HEAD_DIM :, :] = jnp.concatenate(rows, axis=0).astype(BF16)


def combine_kernel(acc_ref, m_ref, text_acc_ref, text_m_ref, *refs):
    packs, (own_ref, other_ref) = refs[:-2], refs[-2:]
    heads, _, mine = text_acc_ref.shape
    columns = []
    for h in range(heads):
        sums = [acc_ref[h, :HEAD_DIM, :mine], text_acc_ref[h, :HEAD_DIM, :]]
        totals = [r[h, HEAD_DIM : HEAD_DIM + 1, :mine] for r in (acc_ref, text_acc_ref)]
        tops = [r[h, 0:1, :mine] for r in (m_ref, text_m_ref)]
        for pack in packs:
            sums.append(pack[h * HEAD_DIM : (h + 1) * HEAD_DIM, :].astype(F32))
            stats = pack[heads * HEAD_DIM :, :].astype(F32)
            at = 6 * h
            totals.append(stats[at : at + 1] + stats[at + 1 : at + 2] + stats[at + 2 : at + 3])
            tops.append(stats[at + 3 : at + 4] + stats[at + 4 : at + 5] + stats[at + 5 : at + 6])
        top = functools.reduce(jnp.maximum, tops)
        shares = [jnp.exp2(t - top) for t in tops]
        total = sum(t * s for t, s in zip(totals, shares))
        mixed = sum(a * s for a, s in zip(sums, shares))
        columns.append(mixed / total)
    rows = jnp.concatenate(columns, axis=0).T.astype(BF16)
    own_ref[...] = rows[: mine // 2]
    other_ref[...] = rows[mine // 2 :]


def out_kernel(row_ref, *refs):
    pieces, w_ref, bias_ref, out_ref = refs[:-3], refs[-3], refs[-2], refs[-1]
    total = jnp.broadcast_to(bias_ref[0:1, :], out_ref.shape)
    for at, piece in enumerate(pieces):
        width = piece.shape[1]
        here = pl.ds(pl.multiple_of(row_ref[at], width), width)
        total = total + jnp.dot(piece[...], w_ref[here, :], preferred_element_type=F32)
    out_ref[...] = total.astype(BF16)


def body(
    image_tokens, text_tokens, w_query_key, w_value, qkv_bias, w_text, text_bias, w_out, out_bias
):
    block, model_width = image_tokens.shape
    local_width = w_value.shape[1]
    width = local_width // 2
    heads = width // HEAD_DIM
    mine = block * X * CORE
    queries = mine * Y
    text_count = text_tokens.shape[0]
    text_rows = -(-text_count // 128) * 128
    blk, uly = lax.axis_index("blk"), lax.axis_index("uly")
    x_high = blk // (Y * Z)
    x_at, core_at = x_high * 2 + uly // CORE, uly % CORE

    with jax.named_scope("tokens"):
        near = [image_tokens] + [fetch(image_tokens, dx=d) for d in (1, -1, 2)]
        own_tokens = jnp.concatenate(near, axis=0)
        other_tokens = fetch(own_tokens, dcore=1)

    with jax.named_scope("weights"):
        def half(array, axis):
            return lax.dynamic_slice_in_dim(array, x_high * width, width, axis)

        pair = half(w_query_key, 2)
        weights = jnp.concatenate([pair[:, 0], pair[:, 1], half(w_value, 1)], axis=1)
        bias = jnp.broadcast_to(half(qkv_bias, 1).reshape(1, 3 * width), (8, 3 * width))
        text_pair = half(w_text, 2)
        text_weights = jnp.concatenate([text_pair[:, 0], text_pair[:, 1]], axis=1)
        text_bias_row = jnp.broadcast_to(half(text_bias, 1).reshape(1, 2 * width), (8, 2 * width))
        padded_text = jnp.pad(text_tokens, ((0, text_rows - text_count), (0, 0)))

    with jax.named_scope("project"):
        text_kv = call(
            functools.partial(text_kernel, text_count),
            shape((heads, 2 * HEAD_DIM, text_rows), BF16),
            4 * text_rows * model_width * width,
            padded_text,
            text_weights,
            text_bias_row,
            name="text_project",
        )
        q_own, kv_own = call(
            project_kernel,
            (shape((heads, HEAD_DIM, mine), BF16), shape((heads, 2 * HEAD_DIM, mine), BF16)),
            6 * mine * model_width * width,
            own_tokens,
            other_tokens,
            weights,
            bias,
            name="project",
        )

    with jax.named_scope("exchange"):
        up = [fetch(kv_own, dz=1)]
        down = [fetch(kv_own, dz=-1)]
        q_parts = [q_own] + [fetch(q_own, dy=d) for d in (1, -1, 2)]
        for _ in range(2):
            up.append(fetch(up[-1], dz=1))
            down.append(fetch(down[-1], dz=-1))
        far_keys = fetch(up[-1][:, :HEAD_DIM], dz=1)
        far_values = fetch(down[-1][:, HEAD_DIM:], dz=-1)
        w_full = lax.all_gather(w_out, "uly", axis=0, tiled=True)

    def state_shapes(count):
        return (
            shape((heads, HEAD_DIM + ONES, count), F32),
            shape((heads, 8, count), F32),
            shape((8, 128), F32),
        )

    def query_shapes(count):
        return (shape((heads, 2 * HEAD_DIM, count), BF16), shape((heads, 8, 128), F32))

    def costs(rows, columns):
        return 4 * heads * rows * columns * 256

    with jax.named_scope("attend"):
        acc, m, _ = state_shapes(mine)
        q2, norm = query_shapes(mine)
        text_acc, text_m, *_ = call(
            functools.partial(text_attend_kernel, text_count),
            (acc, m, q2, norm, shape((8, 128), F32)),
            costs(mine, text_rows),
            q_own,
            text_kv,
            exps=heads * mine * text_rows,
            name="text_attend",
        )
        acc, m, bound, q2, norm = call(
            functools.partial(first_kernel, 3, 768),
            state_shapes(queries) + query_shapes(queries),
            costs(queries, 3 * mine),
            *q_parts,
            kv_own,
            up[0],
            down[0],
            exps=heads * queries * 3 * mine,
            name="attend_first",
        )
        for at in (1, 2):
            acc, m, bound = call(
                functools.partial(next_kernel, 2, 768),
                state_shapes(queries),
                costs(queries, 2 * mine),
                up[at],
                down[at],
                q2,
                norm,
                acc,
                m,
                bound,
                exps=heads * queries * 2 * mine,
                aliases={4: 0, 5: 1, 6: 2},
                name="attend_next",
            )
        pack = shape((heads * HEAD_DIM + STATS, mine), BF16)
        acc, m, _, *packs = call(
            functools.partial(last_kernel, 1536),
            state_shapes(queries) + (pack,) * (Y - 1),
            costs(queries, mine),
            far_keys,
            far_values,
            q2,
            norm,
            acc,
            m,
            bound,
            exps=heads * queries * mine,
            aliases={4: 0, 5: 1, 6: 2},
            name="attend_last",
        )

    with jax.named_scope("combine"):
        returned = [fetch(pack, dy=-d) for pack, d in zip(packs, (1, -1, 2))]
        rows = shape((mine // 2, width), BF16)
        own_rows, other_rows = call(
            combine_kernel, (rows, rows), 0, acc, m, text_acc, text_m, *returned, name="combine"
        )
        sibling_rows = fetch(other_rows, dcore=1)

    with jax.named_scope("output"):
        offsets = (0, 1, -1, 2)
        pieces, places_of = [], []
        for at, d in enumerate(offsets):
            here = slice(at * block, (at + 1) * block)
            both = jnp.concatenate([own_rows[here], sibling_rows[here]], axis=1)
            both = both if d == 0 else fetch(both, dx=-d)
            x_from = lax.rem(x_at - d + X, X)
            for c in range(CORE):
                core_from = lax.rem(core_at + c, CORE)
                pieces.append(both[:, c * width : (c + 1) * width])
                places_of.append(
                    ((x_from % 2) * CORE + core_from) * local_width + (x_from // 2) * width
                )
        rows_at = jnp.stack(places_of).astype(jnp.int32)
        spec = pl.BlockSpec(memory_space=pltpu.VMEM)
        return pl.pallas_call(
            out_kernel,
            out_shape=shape((block, model_width), BF16),
            in_specs=[pl.BlockSpec(memory_space=pltpu.SMEM)] + [spec] * (len(pieces) + 2),
            out_specs=spec,
            compiler_params=pltpu.CompilerParams(vmem_limit_bytes=40 << 20),
            cost_estimate=pl.CostEstimate(
                flops=2 * block * model_width**2, bytes_accessed=2 * model_width**2, transcendentals=0
            ),
            name="output",
        )(rows_at, *pieces, w_full, jnp.broadcast_to(out_bias.reshape(1, -1), (8, model_width)))


def solution(mesh):
    in_specs = (
        P(("uly", "blk"), None),
        P(),
        P(None, None, "uly"),
        P(None, "uly"),
        P(None, "uly"),
        P(None, None, "uly"),
        P(None, "uly"),
        P("uly", None),
        P(),
    )
    out_specs = P(("uly", "blk"), None)
    return jax.shard_map(body, mesh=mesh, in_specs=in_specs, out_specs=out_specs, check_vma=False)
```

```python
import functools

import jax
import jax.numpy as jnp
from jax import lax
from jax.experimental import pallas as pl
from jax.experimental.pallas import tpu as pltpu
from jax.sharding import PartitionSpec as P

HEAD_DIM = 64
AXES = ("uly", "blk")
X, CORE, Y, Z = 4, 2, 4, 8
ONES = 16
VMEM_BYTES = 16 << 20
STATS = 32
LOG2_SCALE = 1.4426950408889634 * HEAD_DIM**-0.5
SAFE_SQUARE = 96.0**2
MASKED = -1e30
BF16, F32 = jnp.bfloat16, jnp.float32


def device_id(x, core, y, z):
    return ((x % 2) * CORE + core) * (2 * Y * Z) + (x // 2) * (Y * Z) + y * Z + z


def places():
    return [
        (x, core, y, z) for x in range(X) for core in range(CORE) for y in range(Y) for z in range(Z)
    ]


def fetch(array, dx=0, dcore=0, dy=0, dz=0):
    pairs = [
        (
            device_id((x + dx) % X, (core + dcore) % CORE, (y + dy) % Y, (z + dz) % Z),
            device_id(x, core, y, z),
        )
        for x, core, y, z in places()
    ]
    return lax.ppermute(array, AXES, pairs)


def call(kernel, out_shape, flops, *operands, exps=0, aliases=None, scratch=(), scalars=(), name=None):
    spec = pl.BlockSpec(memory_space=pltpu.VMEM)
    scalar_spec = pl.BlockSpec(memory_space=pltpu.SMEM)
    moved = sum(a.size * a.dtype.itemsize for a in operands)
    return pl.pallas_call(
        kernel,
        out_shape=out_shape,
        in_specs=[scalar_spec] * len(scalars) + [spec] * len(operands),
        out_specs=jax.tree.map(lambda _: spec, out_shape),
        input_output_aliases=aliases or {},
        scratch_shapes=scratch,
        compiler_params=pltpu.CompilerParams(vmem_limit_bytes=VMEM_BYTES),
        cost_estimate=pl.CostEstimate(flops=flops, bytes_accessed=moved, transcendentals=exps),
        name=name,
    )(*scalars, *operands)


def shape(dims, dtype):
    return jax.ShapeDtypeStruct(dims, dtype)


def halves_kernel(width, high_ref, *refs):
    parts, out_ref = refs[:-1], refs[-1]
    at = 0
    for part in parts:
        for cut in range(0, part.shape[1], 2 * width):
            low, high = part[:, cut : cut + width], part[:, cut + width : cut + 2 * width]
            out_ref[:, at : at + width] = jnp.where(high_ref[0] == 1, high, low)
            at += width


def project_kernel(w_ref, bias_ref, *refs):
    blocks, (q_ref, kv_ref, tokens) = refs[:-3], refs[-3:]
    heads = q_ref.shape[0]
    width = heads * HEAD_DIM
    rows = blocks[0].shape[0]
    for at, block in enumerate(blocks):
        tokens[at * rows : (at + 1) * rows, :] = block[...]
    projected = jnp.dot(tokens[...], w_ref[...], preferred_element_type=F32) + bias_ref[0:1, :]
    columns = projected.T.astype(BF16)
    for h in range(heads):
        cut = h * HEAD_DIM
        q_ref[h] = columns[cut : cut + HEAD_DIM]
        kv_ref[h, :HEAD_DIM, :] = columns[width + cut : width + cut + HEAD_DIM]
        kv_ref[h, HEAD_DIM:, :] = columns[2 * width + cut : 2 * width + cut + HEAD_DIM]


def text_kernel(text_ref, w_ref, bias_ref, kv_ref, rows_ref):
    heads = kv_ref.shape[0]
    width = heads * HEAD_DIM
    count = text_ref.shape[0]
    rows_ref[...] = jnp.zeros_like(rows_ref)
    rows_ref[:count, :] = (
        jnp.dot(text_ref[...], w_ref[...], preferred_element_type=F32) + bias_ref[0:1, :]
    )
    columns = rows_ref[...].T.astype(BF16)
    for h in range(heads):
        cut = h * HEAD_DIM
        kv_ref[h, :HEAD_DIM, :] = columns[cut : cut + HEAD_DIM]
        kv_ref[h, HEAD_DIM:, :] = columns[width + cut : width + cut + HEAD_DIM]


def scale_queries(parts, q2_ref, norm_ref):
    for h in range(q2_ref.shape[0]):
        largest = None
        for at, part in enumerate(parts):
            scaled = part[h].astype(F32) * LOG2_SCALE
            high = scaled.astype(BF16)
            low = (scaled - high.astype(F32)).astype(BF16)
            here = slice(at * part.shape[2], (at + 1) * part.shape[2])
            q2_ref[h, :HEAD_DIM, here] = high
            q2_ref[h, HEAD_DIM:, here] = low
            top = jnp.max(jnp.sum(scaled * scaled, axis=0, keepdims=True), axis=1, keepdims=True)
            largest = top if largest is None else jnp.maximum(largest, top)
        norm_ref[h] = jnp.broadcast_to(largest, norm_ref.shape[1:])


def keys_of(parts, h):
    return jnp.concatenate([k[h, :HEAD_DIM, :] for k, _ in parts], axis=1)


def values_of(parts, h, count):
    values = jnp.concatenate([v[h, -HEAD_DIM:, :] for _, v in parts], axis=1)
    ones = jnp.ones((ONES, values.shape[1]), BF16)
    if count is not None:
        inside = lax.broadcasted_iota(jnp.int32, ones.shape, 1) < count
        ones = jnp.where(inside, 1.0, 0.0).astype(BF16)
    return jnp.concatenate([values, ones], axis=0)


def attend(parts, q2_ref, norm_ref, bound, state_in, acc_ref, m_ref, bound_ref, tile, count=None):
    heads, _, queries = q2_ref.shape
    worst = None
    for h in range(heads):
        keys = keys_of(parts, h).astype(F32)
        top = jnp.max(jnp.sum(keys * keys, axis=0, keepdims=True), axis=1, keepdims=True)
        product = top * norm_ref[h, 0:1, 0:1]
        worst = product if worst is None else jnp.maximum(worst, product)
    if bound is not None:
        worst = jnp.maximum(worst, bound[0:1, 0:1])
    bound_ref[...] = jnp.broadcast_to(worst, bound_ref.shape)
    safe = jnp.max(worst) <= SAFE_SQUARE

    def doubled_keys(h):
        keys = keys_of(parts, h)
        return jnp.concatenate([keys, keys], axis=0).T

    @pl.when(safe)
    def _():
        for h in range(heads):
            keys, values = doubled_keys(h), values_of(parts, h, count)
            for at in range(0, queries, tile):
                here = slice(at, at + tile)
                scores = jnp.dot(keys, q2_ref[h, :, here], preferred_element_type=F32)
                weights = jnp.exp2(scores).astype(BF16)
                term = jnp.dot(values, weights, preferred_element_type=F32)
                acc_ref[h, :, here] = term if state_in is None else state_in[0][h, :, here] + term
        m_ref[...] = jnp.zeros_like(m_ref) if state_in is None else state_in[1][...]

    @pl.when(jnp.logical_not(safe))
    def _():
        step = 128

        def one_head(h, carry):
            keys, values = doubled_keys(h), values_of(parts, h, count)

            def one_tile(at, carry):
                here = pl.ds(pl.multiple_of(at * step, step), step)
                scores = jnp.dot(keys, q2_ref[h, :, here], preferred_element_type=F32)
                if count is not None:
                    inside = lax.broadcasted_iota(jnp.int32, scores.shape, 0) < count
                    scores = jnp.where(inside, scores, MASKED)
                top = jnp.max(scores, axis=0, keepdims=True)
                if state_in is not None:
                    before = state_in[1][h, 0:1, here]
                    top = jnp.maximum(top, before)
                weights = jnp.exp2(scores - top).astype(BF16)
                term = jnp.dot(values, weights, preferred_element_type=F32)
                if state_in is not None:
                    term = term + state_in[0][h, :, here] * jnp.exp2(before - top)
                acc_ref[h, :, here] = term
                m_ref[h, :, here] = jnp.broadcast_to(top, (m_ref.shape[1], step))
                return carry

            return lax.fori_loop(0, queries // step, one_tile, carry)

        lax.fori_loop(0, heads, one_head, 0)


def text_attend_kernel(count, q_ref, kv_ref, acc_ref, m_ref, q2_ref, norm_ref, bound_ref):
    scale_queries([q_ref], q2_ref, norm_ref)
    parts = [(kv_ref, kv_ref)]
    tile = q2_ref.shape[2]
    attend(parts, q2_ref, norm_ref, None, None, acc_ref, m_ref, bound_ref, tile, count)


def first_kernel(n_parts, tile, *refs):
    q_refs, kv_refs = refs[:Y], refs[Y : Y + n_parts]
    acc_ref, m_ref, bound_ref, q2_ref, norm_ref = refs[Y + n_parts :]
    scale_queries(q_refs, q2_ref, norm_ref)
    parts = [(r, r) for r in kv_refs]
    attend(parts, q2_ref, norm_ref, None, None, acc_ref, m_ref, bound_ref, tile)


def next_kernel(n_parts, tile, *refs):
    kv_refs = refs[:n_parts]
    q2_ref, norm_ref, acc_in, m_in, bound_in, acc_ref, m_ref, bound_ref = refs[n_parts:]
    parts = [(r, r) for r in kv_refs]
    attend(parts, q2_ref, norm_ref, bound_in, (acc_in, m_in), acc_ref, m_ref, bound_ref, tile)


def three_parts(value):
    high = value.astype(BF16).astype(F32)
    middle = (value - high).astype(BF16).astype(F32)
    return [high, middle, value - high - middle]


def last_kernel(tile, k_ref, v_ref, *refs):
    q2_ref, norm_ref, acc_in, m_in, bound_in, own_acc, own_m = refs[:7]
    packs, (acc_ref, m_ref, bound_ref) = refs[7:-3], refs[-3:]
    parts = [(k_ref, v_ref)]
    attend(parts, q2_ref, norm_ref, bound_in, (acc_in, m_in), acc_ref, m_ref, bound_ref, tile)
    heads, _, queries = q2_ref.shape
    mine = queries // Y
    own_acc[...] = acc_ref[:, :, :mine]
    own_m[...] = m_ref[:, :, :mine]
    for at, pack in enumerate(packs):
        here = slice((at + 1) * mine, (at + 2) * mine)
        rows = []
        for h in range(heads):
            pack[h * HEAD_DIM : (h + 1) * HEAD_DIM, :] = acc_ref[h, :HEAD_DIM, here].astype(BF16)
            rows += three_parts(acc_ref[h, HEAD_DIM : HEAD_DIM + 1, here])
            rows += three_parts(m_ref[h, 0:1, here])
        rows.append(jnp.zeros((STATS - len(rows), mine), F32))
        pack[heads * HEAD_DIM :, :] = jnp.concatenate(rows, axis=0).astype(BF16)


def combine_kernel(acc_ref, m_ref, text_acc_ref, text_m_ref, *refs):
    packs, (own_ref, other_ref) = refs[:-2], refs[-2:]
    heads, _, mine = acc_ref.shape
    columns = []
    for h in range(heads):
        sums = [acc_ref[h, :HEAD_DIM, :], text_acc_ref[h, :HEAD_DIM, :]]
        totals = [r[h, HEAD_DIM : HEAD_DIM + 1, :] for r in (acc_ref, text_acc_ref)]
        tops = [r[h, 0:1, :] for r in (m_ref, text_m_ref)]
        for pack in packs:
            sums.append(pack[h * HEAD_DIM : (h + 1) * HEAD_DIM, :].astype(F32))
            stats = pack[heads * HEAD_DIM :, :].astype(F32)
            at = 6 * h
            totals.append(stats[at : at + 1] + stats[at + 1 : at + 2] + stats[at + 2 : at + 3])
            tops.append(stats[at + 3 : at + 4] + stats[at + 4 : at + 5] + stats[at + 5 : at + 6])
        top = functools.reduce(jnp.maximum, tops)
        shares = [jnp.exp2(t - top) for t in tops]
        total = sum(t * s for t, s in zip(totals, shares))
        mixed = sum(a * s for a, s in zip(sums, shares))
        columns.append(mixed / total)
    rows = jnp.concatenate(columns, axis=0).T.astype(BF16)
    own_ref[...] = rows[: mine // 2]
    other_ref[...] = rows[mine // 2 :]


def out_kernel(row_ref, start_ref, w_ref, *refs):
    pieces, out_ref = refs[:-1], refs[-1]
    total = jnp.broadcast_to(start_ref[...], out_ref.shape)
    for at, piece in enumerate(pieces):
        width = piece.shape[1]
        here = pl.ds(pl.multiple_of(row_ref[at], width), width)
        total = total + jnp.dot(piece[...], w_ref[here, :], preferred_element_type=F32)
    out_ref[...] = total.astype(out_ref.dtype)


def body(
    image_tokens, text_tokens, w_query_key, w_value, qkv_bias, w_text, text_bias, w_out, out_bias
):
    block, model_width = image_tokens.shape
    local_width = w_value.shape[1]
    width = local_width // 2
    heads = width // HEAD_DIM
    mine = block * X * CORE
    queries = mine * Y
    text_count = text_tokens.shape[0]
    text_rows = -(-text_count // 128) * 128
    blk, uly = lax.axis_index("blk"), lax.axis_index("uly")
    x_high = blk // (Y * Z)
    x_at, core_at = x_high * 2 + uly // CORE, uly % CORE

    with jax.named_scope("tokens"):
        near = [image_tokens] + [fetch(image_tokens, dx=d) for d in (1, -1, 2)]

    with jax.named_scope("weights"):
        high = x_high.reshape(1).astype(jnp.int32)

        def halves(*parts):
            columns = sum(p.shape[1] for p in parts) // 2
            return call(
                functools.partial(halves_kernel, width),
                shape((model_width, columns), BF16),
                0,
                *parts,
                scalars=(high,),
                name="halves",
            )

        def half_row(array):
            half = lax.dynamic_slice_in_dim(array, x_high * width, width, 1).reshape(1, -1)
            return jnp.broadcast_to(half, (8, half.shape[1]))

        text_weights = halves(w_text.reshape(model_width, 2 * local_width))
        weights = halves(w_query_key.reshape(model_width, 2 * local_width), w_value)
        bias, text_bias_row = half_row(qkv_bias), half_row(text_bias)

    with jax.named_scope("project"):
        text_kv = call(
            text_kernel,
            shape((heads, 2 * HEAD_DIM, text_rows), BF16),
            4 * text_rows * model_width * width,
            text_tokens,
            text_weights,
            text_bias_row,
            scratch=[pltpu.VMEM((text_rows, 2 * width), F32)],
            name="text_project",
        )
        near, weights, bias, text_kv = lax.optimization_barrier((near, weights, bias, text_kv))
        blocks = near + [fetch(block_rows, dcore=1) for block_rows in near]
        q_own, kv_own = call(
            project_kernel,
            (shape((heads, HEAD_DIM, mine), BF16), shape((heads, 2 * HEAD_DIM, mine), BF16)),
            6 * mine * model_width * width,
            weights,
            bias,
            *blocks,
            scratch=[pltpu.VMEM((mine, model_width), BF16)],
            name="project",
        )

    with jax.named_scope("exchange"):
        up = [fetch(kv_own, dz=1)]
        down = [fetch(kv_own, dz=-1)]
        q_parts = [q_own] + [fetch(q_own, dy=d) for d in (1, -1, 2)]
        for _ in range(2):
            up.append(fetch(up[-1], dz=1))
            down.append(fetch(down[-1], dz=-1))
        far_keys = fetch(up[-1][:, :HEAD_DIM], dz=1)
        far_values = fetch(down[-1][:, HEAD_DIM:], dz=-1)
        w_full = lax.all_gather(w_out, "uly", axis=0, tiled=True)

    def state_shapes(count):
        return (
            shape((heads, HEAD_DIM + ONES, count), F32),
            shape((heads, 8, count), F32),
            shape((8, 128), F32),
        )

    def query_shapes(count):
        return (shape((heads, 2 * HEAD_DIM, count), BF16), shape((heads, 8, 128), F32))

    def costs(rows, columns):
        return 4 * heads * rows * columns * 256

    with jax.named_scope("attend"):
        acc, m, _ = state_shapes(mine)
        q2, norm = query_shapes(mine)
        text_acc, text_m, *_ = call(
            functools.partial(text_attend_kernel, text_count),
            (acc, m, q2, norm, shape((8, 128), F32)),
            costs(mine, text_rows),
            q_own,
            text_kv,
            exps=heads * mine * text_rows,
            name="text_attend",
        )
        text_acc, text_m, q_parts = lax.optimization_barrier((text_acc, text_m, q_parts))
        acc, m, bound, q2, norm = call(
            functools.partial(first_kernel, 3, 768),
            state_shapes(queries) + query_shapes(queries),
            costs(queries, 3 * mine),
            *q_parts,
            kv_own,
            up[0],
            down[0],
            exps=heads * queries * 3 * mine,
            name="attend_first",
        )
        for at in (1, 2):
            acc, m, bound = call(
                functools.partial(next_kernel, 2, 768),
                state_shapes(queries),
                costs(queries, 2 * mine),
                up[at],
                down[at],
                q2,
                norm,
                acc,
                m,
                bound,
                exps=heads * queries * 2 * mine,
                aliases={4: 0, 5: 1, 6: 2},
                name="attend_next",
            )
        pack = shape((heads * HEAD_DIM + STATS, mine), BF16)
        acc, m, *packs = call(
            functools.partial(last_kernel, 1536),
            state_shapes(mine)[:2] + (pack,) * (Y - 1),
            costs(queries, mine),
            far_keys,
            far_values,
            q2,
            norm,
            acc,
            m,
            bound,
            exps=heads * queries * mine,
            scratch=[pltpu.VMEM(s.shape, s.dtype) for s in state_shapes(queries)],
            name="attend_last",
        )

    with jax.named_scope("combine"):
        returned = [fetch(pack, dy=-d) for pack, d in zip(packs, (1, -1, 2))]
        rows = shape((mine // 2, width), BF16)
        own_rows, other_rows = call(
            combine_kernel, (rows, rows), 0, acc, m, text_acc, text_m, *returned, name="combine"
        )
        sibling_rows = fetch(other_rows, dcore=1)

    with jax.named_scope("output"):

        def rows_from(d):
            x_from = lax.rem(x_at - d + X, X)
            cores = [core_at, CORE - 1 - core_at]
            return [
                ((x_from % 2) * CORE + c) * local_width + (x_from // 2) * width for c in cores
            ]

        def multiply(start, pieces, distances, dtype, name):
            rows_at = jnp.stack([r for d in distances for r in rows_from(d)]).astype(jnp.int32)
            return call(
                out_kernel,
                shape((block, model_width), dtype),
                2 * block * model_width * width * len(pieces),
                start,
                w_full,
                *pieces,
                scalars=(rows_at,),
                name=name,
            )

        far, both = (1, -1, 2), []
        for at, d in enumerate(far, 1):
            here = slice(at * block, (at + 1) * block)
            sent = jnp.concatenate([own_rows[here], sibling_rows[here]], axis=1)
            both.append(fetch(sent, dx=-d))
        near_pieces = [own_rows[:block], sibling_rows[:block]]
        start = multiply(out_bias.reshape(1, -1), near_pieces, (0,), F32, "output_near")
        start, both = lax.optimization_barrier((start, both))
        pieces = [b[:, c * width : (c + 1) * width] for b in both for c in range(CORE)]
        return multiply(start, pieces, far, BF16, "output_far")


def solution(mesh):
    in_specs = (
        P(("uly", "blk"), None),
        P(),
        P(None, None, "uly"),
        P(None, "uly"),
        P(None, "uly"),
        P(None, None, "uly"),
        P(None, "uly"),
        P("uly", None),
        P(),
    )
    out_specs = P(("uly", "blk"), None)
    return jax.shard_map(body, mesh=mesh, in_specs=in_specs, out_specs=out_specs, check_vma=False)
```

```python
import functools

import jax
import jax.numpy as jnp
from jax import lax
from jax.experimental import pallas as pl
from jax.experimental.pallas import tpu as pltpu
from jax.sharding import PartitionSpec as P

HEAD_DIM = 64
AXES = ("uly", "blk")
X, CORE, Y, Z = 4, 2, 4, 8
ONES = 16
VMEM_BYTES = 16 << 20
STATS = 32
LOG2_SCALE = 1.4426950408889634 * HEAD_DIM**-0.5
SAFE_SQUARE = 96.0**2
MASKED = -1e30
BF16, F32 = jnp.bfloat16, jnp.float32


def device_id(x, core, y, z):
    return ((x % 2) * CORE + core) * (2 * Y * Z) + (x // 2) * (Y * Z) + y * Z + z


def places():
    return [
        (x, core, y, z) for x in range(X) for core in range(CORE) for y in range(Y) for z in range(Z)
    ]


def fetch(array, dx=0, dcore=0, dy=0, dz=0):
    pairs = [
        (
            device_id((x + dx) % X, (core + dcore) % CORE, (y + dy) % Y, (z + dz) % Z),
            device_id(x, core, y, z),
        )
        for x, core, y, z in places()
    ]
    return lax.ppermute(array, AXES, pairs)


def fetch_x_low(array):
    pairs = [
        (device_id(x, core, y, z), device_id(x ^ 1, core, y, z)) for x, core, y, z in places()
    ]
    return lax.ppermute(array, AXES, pairs)


def call(kernel, out_shape, flops, *operands, exps=0, aliases=None, scratch=(), scalars=(), name=None):
    spec = pl.BlockSpec(memory_space=pltpu.VMEM)
    scalar_spec = pl.BlockSpec(memory_space=pltpu.SMEM)
    moved = sum(a.size * a.dtype.itemsize for a in operands)
    return pl.pallas_call(
        kernel,
        out_shape=out_shape,
        in_specs=[scalar_spec] * len(scalars) + [spec] * len(operands),
        out_specs=jax.tree.map(lambda _: spec, out_shape),
        input_output_aliases=aliases or {},
        scratch_shapes=scratch,
        compiler_params=pltpu.CompilerParams(vmem_limit_bytes=VMEM_BYTES),
        cost_estimate=pl.CostEstimate(flops=flops, bytes_accessed=moved, transcendentals=exps),
        name=name,
    )(*scalars, *operands)


def shape(dims, dtype):
    return jax.ShapeDtypeStruct(dims, dtype)


def halves_kernel(width, high_ref, *refs):
    parts, out_ref = refs[:-1], refs[-1]
    at = 0
    for part in parts:
        for cut in range(0, part.shape[1], 2 * width):
            low, high = part[:, cut : cut + width], part[:, cut + width : cut + 2 * width]
            out_ref[:, at : at + width] = jnp.where(high_ref[0] == 1, high, low)
            at += width


def half_row(high_ref, bias_ref, width):
    halves = [
        jnp.where(high_ref[0] == 1, bias_ref[at : at + 1, width:], bias_ref[at : at + 1, :width])
        for at in range(bias_ref.shape[0])
    ]
    return jnp.concatenate(halves, axis=1)


def project_kernel(high_ref, w_ref, bias_ref, *refs):
    blocks, (q_ref, kv_ref, tokens) = refs[:-3], refs[-3:]
    heads = q_ref.shape[0]
    width = heads * HEAD_DIM
    rows = blocks[0].shape[0]
    for at, block in enumerate(blocks):
        tokens[at * rows : (at + 1) * rows, :] = block[...]
    projected = jnp.dot(tokens[...], w_ref[...], preferred_element_type=F32)
    projected = projected + half_row(high_ref, bias_ref, width)
    columns = projected.T.astype(BF16)
    for h in range(heads):
        cut = h * HEAD_DIM
        q_ref[h] = columns[cut : cut + HEAD_DIM]
        kv_ref[h, :HEAD_DIM, :] = columns[width + cut : width + cut + HEAD_DIM]
        kv_ref[h, HEAD_DIM:, :] = columns[2 * width + cut : 2 * width + cut + HEAD_DIM]


def text_kernel(high_ref, text_ref, w_ref, bias_ref, kv_ref, rows_ref):
    heads = kv_ref.shape[0]
    width = heads * HEAD_DIM
    count = text_ref.shape[0]
    rows_ref[...] = jnp.zeros_like(rows_ref)
    rows = jnp.dot(text_ref[...], w_ref[...], preferred_element_type=F32)
    rows_ref[:count, :] = rows + half_row(high_ref, bias_ref, width)
    columns = rows_ref[...].T.astype(BF16)
    for h in range(heads):
        cut = h * HEAD_DIM
        kv_ref[h, :HEAD_DIM, :] = columns[cut : cut + HEAD_DIM]
        kv_ref[h, HEAD_DIM:, :] = columns[width + cut : width + cut + HEAD_DIM]


def scale_queries(parts, q2_ref, norm_ref):
    for h in range(q2_ref.shape[0]):
        largest = None
        for at, part in enumerate(parts):
            scaled = part[h].astype(F32) * LOG2_SCALE
            high = scaled.astype(BF16)
            low = (scaled - high.astype(F32)).astype(BF16)
            here = slice(at * part.shape[2], (at + 1) * part.shape[2])
            q2_ref[h, :HEAD_DIM, here] = high
            q2_ref[h, HEAD_DIM:, here] = low
            top = jnp.max(jnp.sum(scaled * scaled, axis=0, keepdims=True), axis=1, keepdims=True)
            largest = top if largest is None else jnp.maximum(largest, top)
        norm_ref[h] = jnp.broadcast_to(largest, norm_ref.shape[1:])


def keys_of(parts, h):
    return jnp.concatenate([k[h, :HEAD_DIM, :] for k, _ in parts], axis=1)


def values_of(parts, h, count):
    values = jnp.concatenate([v[h, -HEAD_DIM:, :] for _, v in parts], axis=1)
    ones = jnp.ones((ONES, values.shape[1]), BF16)
    if count is not None:
        inside = lax.broadcasted_iota(jnp.int32, ones.shape, 1) < count
        ones = jnp.where(inside, 1.0, 0.0).astype(BF16)
    return jnp.concatenate([values, ones], axis=0)


def attend(parts, text, q2_ref, norm_ref, bound, state_in, acc_ref, m_ref, bound_ref, tile):
    heads, _, queries = q2_ref.shape
    worst = None
    for h in range(heads):
        top = None
        for some in (parts, text[0]) if text else (parts,):
            keys = keys_of(some, h).astype(F32)
            one = jnp.max(jnp.sum(keys * keys, axis=0, keepdims=True), axis=1, keepdims=True)
            top = one if top is None else jnp.maximum(top, one)
        product = top * norm_ref[h, 0:1, 0:1]
        worst = product if worst is None else jnp.maximum(worst, product)
    if bound is not None:
        worst = jnp.maximum(worst, bound[0:1, 0:1])
    bound_ref[...] = jnp.broadcast_to(worst, bound_ref.shape)
    safe = jnp.max(worst) <= SAFE_SQUARE

    def doubled_keys(some, h):
        keys = keys_of(some, h)
        return jnp.concatenate([keys, keys], axis=0).T

    @pl.when(safe)
    def _():
        def visit(some, count, h, here, before):
            scores = jnp.dot(doubled_keys(some, h), q2_ref[h, :, here], preferred_element_type=F32)
            weights = jnp.exp2(scores).astype(BF16)
            term = jnp.dot(values_of(some, h, count), weights, preferred_element_type=F32)
            acc_ref[h, :, here] = term if before is None else before[h, :, here] + term

        for h in range(heads):
            for at in range(0, queries, tile):
                visit(parts, None, h, slice(at, at + tile), state_in and state_in[0])
            if text:
                visit(*text, h, slice(0, queries // Y), acc_ref)
        m_ref[...] = jnp.zeros_like(m_ref) if state_in is None else state_in[1][...]

    @pl.when(jnp.logical_not(safe))
    def _():
        step = 128

        def pass_over(some, count, queries, before):
            def one_head(h, carry):
                keys, values = doubled_keys(some, h), values_of(some, h, count)

                def one_tile(at, carry):
                    here = pl.ds(pl.multiple_of(at * step, step), step)
                    scores = jnp.dot(keys, q2_ref[h, :, here], preferred_element_type=F32)
                    if count is not None:
                        inside = lax.broadcasted_iota(jnp.int32, scores.shape, 0) < count
                        scores = jnp.where(inside, scores, MASKED)
                    top = jnp.max(scores, axis=0, keepdims=True)
                    if before is not None:
                        old = before[1][h, 0:1, here]
                        top = jnp.maximum(top, old)
                    weights = jnp.exp2(scores - top).astype(BF16)
                    term = jnp.dot(values, weights, preferred_element_type=F32)
                    if before is not None:
                        term = term + before[0][h, :, here] * jnp.exp2(old - top)
                    acc_ref[h, :, here] = term
                    m_ref[h, :, here] = jnp.broadcast_to(top, (m_ref.shape[1], step))
                    return carry

                return lax.fori_loop(0, queries // step, one_tile, carry)

            lax.fori_loop(0, heads, one_head, 0)

        pass_over(parts, None, queries, state_in)
        if text:
            pass_over(*text, queries // Y, (acc_ref, m_ref))


def first_kernel(n_parts, tile, *refs):
    q_refs, kv_refs = refs[:Y], refs[Y : Y + n_parts]
    acc_ref, m_ref, bound_ref, q2_ref, norm_ref = refs[Y + n_parts :]
    scale_queries(q_refs, q2_ref, norm_ref)
    parts = [(r, r) for r in kv_refs]
    attend(parts, None, q2_ref, norm_ref, None, None, acc_ref, m_ref, bound_ref, tile)


def next_kernel(n_parts, tile, count, *refs):
    kv_refs, refs = refs[:n_parts], refs[n_parts:]
    text = None
    if count:
        text, refs = ([(refs[0], refs[0])], count), refs[1:]
    q2_ref, norm_ref, acc_in, m_in, bound_in, acc_ref, m_ref, bound_ref = refs
    parts = [(r, r) for r in kv_refs]
    state = (acc_in, m_in)
    attend(parts, text, q2_ref, norm_ref, bound_in, state, acc_ref, m_ref, bound_ref, tile)


def three_parts(value):
    high = value.astype(BF16).astype(F32)
    middle = (value - high).astype(BF16).astype(F32)
    return [high, middle, value - high - middle]


def last_kernel(tile, k_ref, v_ref, *refs):
    q2_ref, norm_ref, acc_in, m_in, bound_in, own_acc, own_m = refs[:7]
    packs, (acc_ref, m_ref, bound_ref) = refs[7:-3], refs[-3:]
    parts = [(k_ref, v_ref)]
    state = (acc_in, m_in)
    attend(parts, None, q2_ref, norm_ref, bound_in, state, acc_ref, m_ref, bound_ref, tile)
    heads, _, queries = q2_ref.shape
    mine = queries // Y
    own_acc[...] = acc_ref[:, :, :mine]
    own_m[...] = m_ref[:, :, :mine]
    for at, pack in enumerate(packs):
        here = slice((at + 1) * mine, (at + 2) * mine)
        rows = []
        for h in range(heads):
            pack[h * HEAD_DIM : (h + 1) * HEAD_DIM, :] = acc_ref[h, :HEAD_DIM, here].astype(BF16)
            rows += three_parts(acc_ref[h, HEAD_DIM : HEAD_DIM + 1, here])
            rows += three_parts(m_ref[h, 0:1, here])
        rows.append(jnp.zeros((STATS - len(rows), mine), F32))
        pack[heads * HEAD_DIM :, :] = jnp.concatenate(rows, axis=0).astype(BF16)


def combine_kernel(odd_ref, acc_ref, m_ref, *refs):
    packs, (kept_ref, sent_ref) = refs[:-2], refs[-2:]
    heads, _, mine = acc_ref.shape
    columns = []
    for h in range(heads):
        sums = [acc_ref[h, :HEAD_DIM, :]]
        totals = [acc_ref[h, HEAD_DIM : HEAD_DIM + 1, :]]
        tops = [m_ref[h, 0:1, :]]
        for pack in packs:
            sums.append(pack[h * HEAD_DIM : (h + 1) * HEAD_DIM, :].astype(F32))
            stats = pack[heads * HEAD_DIM :, :].astype(F32)
            at = 6 * h
            totals.append(stats[at : at + 1] + stats[at + 1 : at + 2] + stats[at + 2 : at + 3])
            tops.append(stats[at + 3 : at + 4] + stats[at + 4 : at + 5] + stats[at + 5 : at + 6])
        top = functools.reduce(jnp.maximum, tops)
        shares = [jnp.exp2(t - top) for t in tops]
        total = sum(t * s for t, s in zip(totals, shares))
        mixed = sum(a * s for a, s in zip(sums, shares))
        columns.append(mixed / total)
    rows = jnp.concatenate(columns, axis=0).T.astype(BF16)
    block = mine // (X * CORE)
    for core in range(CORE):
        here, up, down, far = [
            rows[(core * X + at) * block : (core * X + at + 1) * block] for at in range(X)
        ]
        at = 2 * core * block
        kept_ref[at : at + block, :] = here
        sent_ref[at : at + block, :] = far
        kept_ref[at + block : at + 2 * block, :] = jnp.where(odd_ref[0] == 1, down, up)
        sent_ref[at + block : at + 2 * block, :] = jnp.where(odd_ref[0] == 1, up, down)


def out_rows(rows_ref, w_ref, half):
    width = rows_ref.shape[1]
    here = pl.ds(pl.multiple_of(half * width, width), width)
    return jnp.dot(rows_ref[...], w_ref[here, :], preferred_element_type=F32)


def near_kernel(high_ref, rows_ref, w_ref, out_ref):
    out_ref[...] = out_rows(rows_ref, w_ref, high_ref[0])


def far_kernel(high_ref, rows_ref, w_ref, near_ref, kept_ref, sent_ref):
    total = near_ref[...] + out_rows(rows_ref, w_ref, 1 - high_ref[0])
    half = kept_ref.shape[0]
    kept_ref[...] = total[:half]
    sent_ref[...] = total[half:].astype(BF16)


def add_kernel(kept_in, received_ref, kept_ref, sent_ref):
    total = kept_in[...] + received_ref[...].astype(F32)
    half = kept_ref.shape[0]
    kept_ref[...] = total[:half]
    sent_ref[...] = total[half:].astype(BF16)


def finish_kernel(kept_ref, received_ref, bias_ref, out_ref):
    out_ref[...] = (kept_ref[...] + received_ref[...].astype(F32) + bias_ref[...]).astype(BF16)


def body(
    image_tokens, text_tokens, w_query_key, w_value, qkv_bias, w_text, text_bias, w_out, out_bias
):
    block, model_width = image_tokens.shape
    local_width = w_value.shape[1]
    width = local_width // 2
    heads = width // HEAD_DIM
    mine = block * X * CORE
    queries = mine * Y
    text_count = text_tokens.shape[0]
    text_rows = -(-text_count // 128) * 128
    blk, uly = lax.axis_index("blk"), lax.axis_index("uly")
    x_high = blk // (Y * Z)
    x_at, core_at = x_high * 2 + uly // CORE, uly % CORE

    with jax.named_scope("tokens"):
        near = [image_tokens] + [fetch(image_tokens, dx=d) for d in (1, -1, 2)]

    with jax.named_scope("weights"):
        high = x_high.reshape(1).astype(jnp.int32)

        def halves(*parts):
            columns = sum(p.shape[1] for p in parts) // 2
            return call(
                functools.partial(halves_kernel, width),
                shape((model_width, columns), BF16),
                0,
                *parts,
                scalars=(high,),
                name="halves",
            )

        weights = halves(w_query_key.reshape(model_width, 2 * local_width), w_value)

    with jax.named_scope("project"):
        sibling = fetch(image_tokens, dcore=1)
        near, weights = lax.optimization_barrier((near, weights))
        blocks = near + [sibling] + [fetch(block_rows, dcore=1) for block_rows in near[1:]]
        q_own, kv_own = call(
            project_kernel,
            (shape((heads, HEAD_DIM, mine), BF16), shape((heads, 2 * HEAD_DIM, mine), BF16)),
            6 * mine * model_width * width,
            weights,
            qkv_bias,
            *blocks,
            scalars=(high,),
            scratch=[pltpu.VMEM((mine, model_width), BF16)],
            name="project",
        )
    with jax.named_scope("exchange"):
        up = [fetch(kv_own, dz=1)]
        down = [fetch(kv_own, dz=-1)]
        w_text, up[0] = lax.optimization_barrier((w_text, up[0]))
        text_kv = call(
            text_kernel,
            shape((heads, 2 * HEAD_DIM, text_rows), BF16),
            4 * text_rows * model_width * width,
            text_tokens,
            halves(w_text.reshape(model_width, 2 * local_width)),
            text_bias,
            scalars=(high,),
            scratch=[pltpu.VMEM((text_rows, 2 * width), F32)],
            name="text_project",
        )
        q_parts = [q_own] + [fetch(q_own, dy=d) for d in (1, -1, 2)]
        for _ in range(2):
            up.append(fetch(up[-1], dz=1))
            down.append(fetch(down[-1], dz=-1))
        far_keys = fetch(up[-1][:, :HEAD_DIM], dz=1)
        far_values = fetch(down[-1][:, HEAD_DIM:], dz=-1)

    def state_shapes(count):
        return (
            shape((heads, HEAD_DIM + ONES, count), F32),
            shape((heads, 8, count), F32),
            shape((8, 128), F32),
        )

    def query_shapes(count):
        return (shape((heads, 2 * HEAD_DIM, count), BF16), shape((heads, 8, 128), F32))

    def costs(rows, columns):
        return 2500 * heads * rows * columns

    with jax.named_scope("attend"):
        acc, m, bound, q2, norm = call(
            functools.partial(first_kernel, 3, 768),
            state_shapes(queries) + query_shapes(queries),
            costs(queries, 3 * mine),
            *q_parts,
            kv_own,
            up[0],
            down[0],
            exps=0,
            name="attend_first",
        )
        for at in (1, 2):
            extra = [text_kv] if at == 1 else []
            acc, m, bound = call(
                functools.partial(next_kernel, 2, 768, text_count if extra else None),
                state_shapes(queries),
                costs(queries, 2 * mine),
                up[at],
                down[at],
                *extra,
                q2,
                norm,
                acc,
                m,
                bound,
                exps=0,
                aliases={n + 4 + len(extra): n for n in range(3)},
                name="attend_next",
            )
        pack = shape((heads * HEAD_DIM + STATS, mine), BF16)
        acc, m, *packs = call(
            functools.partial(last_kernel, 1536),
            state_shapes(mine)[:2] + (pack,) * (Y - 1),
            costs(queries, mine),
            far_keys,
            far_values,
            q2,
            norm,
            acc,
            m,
            bound,
            exps=0,
            scratch=[pltpu.VMEM(s.shape, s.dtype) for s in state_shapes(queries)],
            name="attend_last",
        )

    with jax.named_scope("combine"):
        returned = [fetch(pack, dy=-d) for pack, d in zip(packs, (1, -1, 2))]
        rows = shape((mine // 2, width), BF16)
        odd = (x_at % 2).reshape(1).astype(jnp.int32)
        kept, sent = call(
            combine_kernel, (rows, rows), 0, acc, m, *returned, scalars=(odd,), name="combine"
        )

    with jax.named_scope("output"):
        received = fetch(sent, dx=2)
        flops = mine * width * model_width
        near_sum = call(
            near_kernel,
            shape((mine // 2, model_width), F32),
            flops,
            kept,
            w_out,
            scalars=(high,),
            name="output_near",
        )
        received, near_sum = lax.optimization_barrier((received, near_sum))

        def split(rows):
            return (shape((rows, model_width), F32), shape((rows, model_width), BF16))

        kept, sent = call(
            far_kernel,
            split(mine // 4),
            flops,
            received,
            w_out,
            near_sum,
            scalars=(high,),
            name="output_far",
        )
        kept, sent = call(add_kernel, split(block), 0, kept, fetch(sent, dcore=1), name="add_cores")
        return call(
            finish_kernel,
            shape((block, model_width), BF16),
            0,
            kept,
            fetch_x_low(sent),
            out_bias.reshape(1, -1),
            name="finish",
        )


def solution(mesh):
    in_specs = (
        P(("uly", "blk"), None),
        P(),
        P(None, None, "uly"),
        P(None, "uly"),
        P(None, "uly"),
        P(None, None, "uly"),
        P(None, "uly"),
        P("uly", None),
        P(),
    )
    out_specs = P(("uly", "blk"), None)
    return jax.shard_map(body, mesh=mesh, in_specs=in_specs, out_specs=out_specs, check_vma=False)
```

```python
import functools

import jax
import jax.numpy as jnp
from jax import lax
from jax.experimental import pallas as pl
from jax.experimental.pallas import tpu as pltpu
from jax.sharding import PartitionSpec as P

HEAD_DIM = 64
AXES = ("uly", "blk")
X, CORE, Y, Z = 4, 2, 4, 8
ONES = 16
VMEM_BYTES = 16 << 20
STATS = 16
LOG2_SCALE = 1.4426950408889634 * HEAD_DIM**-0.5
SAFE_SQUARE = 96.0**2
MASKED = -1e30
BF16, F32 = jnp.bfloat16, jnp.float32


def device_id(x, core, y, z):
    return ((x % 2) * CORE + core) * (2 * Y * Z) + (x // 2) * (Y * Z) + y * Z + z


def places():
    return [
        (x, core, y, z) for x in range(X) for core in range(CORE) for y in range(Y) for z in range(Z)
    ]


def fetch(array, dx=0, dcore=0, dy=0, dz=0):
    pairs = [
        (
            device_id((x + dx) % X, (core + dcore) % CORE, (y + dy) % Y, (z + dz) % Z),
            device_id(x, core, y, z),
        )
        for x, core, y, z in places()
    ]
    return lax.ppermute(array, AXES, pairs)


def fetch_x_low(array):
    pairs = [
        (device_id(x, core, y, z), device_id(x ^ 1, core, y, z)) for x, core, y, z in places()
    ]
    return lax.ppermute(array, AXES, pairs)


def call(kernel, out_shape, flops, *operands, exps=0, aliases=None, scratch=(), scalars=(), name=None):
    spec = pl.BlockSpec(memory_space=pltpu.VMEM)
    scalar_spec = pl.BlockSpec(memory_space=pltpu.SMEM)
    moved = sum(a.size * a.dtype.itemsize for a in operands)
    return pl.pallas_call(
        kernel,
        out_shape=out_shape,
        in_specs=[scalar_spec] * len(scalars) + [spec] * len(operands),
        out_specs=jax.tree.map(lambda _: spec, out_shape),
        input_output_aliases=aliases or {},
        scratch_shapes=scratch,
        compiler_params=pltpu.CompilerParams(vmem_limit_bytes=VMEM_BYTES),
        cost_estimate=pl.CostEstimate(flops=flops, bytes_accessed=moved, transcendentals=exps),
        name=name,
    )(*scalars, *operands)


def shape(dims, dtype):
    return jax.ShapeDtypeStruct(dims, dtype)


def halves_kernel(width, high_ref, *refs):
    parts, out_ref = refs[:-1], refs[-1]
    at = 0
    for part in parts:
        for cut in range(0, part.shape[1], 2 * width):
            low, high = part[:, cut : cut + width], part[:, cut + width : cut + 2 * width]
            out_ref[:, at : at + width] = jnp.where(high_ref[0] == 1, high, low)
            at += width


def half_row(high_ref, bias_ref, row_ref):
    width = bias_ref.shape[1] // 2
    for at in range(bias_ref.shape[0]):
        low, high = bias_ref[at : at + 1, :width], bias_ref[at : at + 1, width:]
        row_ref[0:1, at * width : (at + 1) * width] = jnp.where(high_ref[0] == 1, high, low)
    return row_ref[0:1, :]


def project_kernel(high_ref, w_ref, bias_ref, *refs):
    blocks, (q_ref, kv_ref, tokens, row_ref) = refs[:-4], refs[-4:]
    heads = q_ref.shape[0]
    width = heads * HEAD_DIM
    rows = blocks[0].shape[0]
    for at, block in enumerate(blocks):
        tokens[at * rows : (at + 1) * rows, :] = block[...]
    projected = jnp.dot(tokens[...], w_ref[...], preferred_element_type=F32)
    projected = projected + half_row(high_ref, bias_ref, row_ref)
    columns = projected.T.astype(BF16)
    for h in range(heads):
        cut = h * HEAD_DIM
        q_ref[h] = columns[cut : cut + HEAD_DIM]
        kv_ref[h, :HEAD_DIM, :] = columns[width + cut : width + cut + HEAD_DIM]
        kv_ref[h, HEAD_DIM:, :] = columns[2 * width + cut : 2 * width + cut + HEAD_DIM]


def text_kernel(high_ref, text_ref, w_ref, bias_ref, kv_ref, rows_ref, row_ref):
    heads = kv_ref.shape[0]
    width = heads * HEAD_DIM
    count = text_ref.shape[0]
    rows_ref[...] = jnp.zeros_like(rows_ref)
    rows = jnp.dot(text_ref[...], w_ref[...], preferred_element_type=F32)
    rows_ref[:count, :] = rows + half_row(high_ref, bias_ref, row_ref)
    columns = rows_ref[...].T.astype(BF16)
    for h in range(heads):
        cut = h * HEAD_DIM
        kv_ref[h, :HEAD_DIM, :] = columns[cut : cut + HEAD_DIM]
        kv_ref[h, HEAD_DIM:, :] = columns[width + cut : width + cut + HEAD_DIM]


def scale_queries(parts, q2_ref, norm_ref):
    for h in range(q2_ref.shape[0]):
        largest = None
        for at, part in enumerate(parts):
            scaled = part[h].astype(F32) * LOG2_SCALE
            high = scaled.astype(BF16)
            low = (scaled - high.astype(F32)).astype(BF16)
            here = slice(at * part.shape[2], (at + 1) * part.shape[2])
            q2_ref[h, :HEAD_DIM, here] = high
            q2_ref[h, HEAD_DIM:, here] = low
            top = jnp.max(jnp.sum(scaled * scaled, axis=0, keepdims=True), axis=1, keepdims=True)
            largest = top if largest is None else jnp.maximum(largest, top)
        norm_ref[h] = jnp.broadcast_to(largest, norm_ref.shape[1:])


def keys_of(parts, h):
    return jnp.concatenate([k[h, :HEAD_DIM, :] for k, _ in parts], axis=1)


def values_of(parts, h, count):
    values = jnp.concatenate([v[h, -HEAD_DIM:, :] for _, v in parts], axis=1)
    ones = jnp.ones((ONES, values.shape[1]), BF16)
    if count is not None:
        inside = lax.broadcasted_iota(jnp.int32, ones.shape, 1) < count
        ones = jnp.where(inside, 1.0, 0.0).astype(BF16)
    return jnp.concatenate([values, ones], axis=0)


def attend(parts, q2_ref, norm_ref, bound, state_in, acc_ref, m_ref, bound_ref, tile, count=None):
    heads, _, queries = acc_ref.shape
    worst = None
    for h in range(heads):
        keys = keys_of(parts, h).astype(F32)
        top = jnp.max(jnp.sum(keys * keys, axis=0, keepdims=True), axis=1, keepdims=True)
        product = top * norm_ref[h, 0:1, 0:1]
        worst = product if worst is None else jnp.maximum(worst, product)
    if bound is not None:
        worst = jnp.maximum(worst, bound[0:1, 0:1])
    bound_ref[...] = jnp.broadcast_to(worst, bound_ref.shape)
    safe = jnp.max(worst) <= SAFE_SQUARE

    def doubled_keys(h):
        keys = keys_of(parts, h)
        return jnp.concatenate([keys, keys], axis=0).T

    @pl.when(safe)
    def _():
        def one_head(h, carry):
            keys, values = doubled_keys(h), values_of(parts, h, count)
            for at in range(0, queries, tile):
                here = slice(at, at + tile)
                scores = jnp.dot(keys, q2_ref[h, :, here], preferred_element_type=F32)
                weights = jnp.exp2(scores).astype(BF16)
                term = jnp.dot(values, weights, preferred_element_type=F32)
                acc_ref[h, :, here] = term if state_in is None else state_in[0][h, :, here] + term
            return carry

        lax.fori_loop(0, heads, one_head, 0)
        m_ref[...] = jnp.zeros_like(m_ref) if state_in is None else state_in[1][...]

    @pl.when(jnp.logical_not(safe))
    def _():
        step = 128

        def one_head(h, carry):
            keys, values = doubled_keys(h), values_of(parts, h, count)

            def one_tile(at, carry):
                here = pl.ds(pl.multiple_of(at * step, step), step)
                scores = jnp.dot(keys, q2_ref[h, :, here], preferred_element_type=F32)
                if count is not None:
                    inside = lax.broadcasted_iota(jnp.int32, scores.shape, 0) < count
                    scores = jnp.where(inside, scores, MASKED)
                top = jnp.max(scores, axis=0, keepdims=True)
                if state_in is not None:
                    before = state_in[1][h, 0:1, here]
                    top = jnp.maximum(top, before)
                weights = jnp.exp2(scores - top).astype(BF16)
                term = jnp.dot(values, weights, preferred_element_type=F32)
                if state_in is not None:
                    term = term + state_in[0][h, :, here] * jnp.exp2(before - top)
                acc_ref[h, :, here] = term
                m_ref[h, :, here] = jnp.broadcast_to(top, (m_ref.shape[1], step))
                return carry

            return lax.fori_loop(0, queries // step, one_tile, carry)

        lax.fori_loop(0, heads, one_head, 0)


def first_kernel(n_parts, tile, *refs):
    q_refs, kv_refs = refs[:Y], refs[Y : Y + n_parts]
    acc_ref, m_ref, bound_ref, q2_ref, norm_ref = refs[Y + n_parts :]
    scale_queries(q_refs, q2_ref, norm_ref)
    parts = [(r, r) for r in kv_refs]
    attend(parts, q2_ref, norm_ref, None, None, acc_ref, m_ref, bound_ref, tile)


def next_kernel(n_parts, tile, count, *refs):
    kv_refs, refs = refs[:n_parts], refs[n_parts:]
    q2_ref, norm_ref, acc_in, m_in, bound_in, acc_ref, m_ref, bound_ref = refs
    parts = [(r, r) for r in kv_refs]
    state = (acc_in, m_in)
    attend(parts, q2_ref, norm_ref, bound_in, state, acc_ref, m_ref, bound_ref, tile, count)


def in_parts(value, count):
    parts = []
    for _ in range(count):
        parts.append(value.astype(BF16).astype(F32))
        value = value - parts[-1]
    return parts


def last_kernel(tile, k_ref, v_ref, *refs):
    q2_ref, norm_ref, acc_in, m_in, bound_in, own_acc, own_m, bound_ref = refs[:8]
    packs, (acc_ref, m_ref) = refs[8:-2], refs[-2:]
    parts = [(k_ref, v_ref)]
    state = (acc_in, m_in)
    attend(parts, q2_ref, norm_ref, bound_in, state, acc_ref, m_ref, bound_ref, tile)
    heads, _, queries = q2_ref.shape
    mine = queries // Y
    own_acc[...] = acc_ref[:, :, :mine]
    own_m[...] = m_ref[:, :, :mine]
    for at, pack in enumerate(packs):
        here = slice((at + 1) * mine, (at + 2) * mine)
        rows = []
        for h in range(heads):
            pack[h * HEAD_DIM : (h + 1) * HEAD_DIM, :] = acc_ref[h, :HEAD_DIM, here].astype(BF16)
            rows += in_parts(acc_ref[h, HEAD_DIM : HEAD_DIM + 1, here], 2)
            rows += in_parts(m_ref[h, 0:1, here], 3)
        rows.append(jnp.zeros((STATS - len(rows), mine), F32))
        pack[heads * HEAD_DIM :, :] = jnp.concatenate(rows, axis=0).astype(BF16)


def combine_kernel(acc_ref, m_ref, *refs):
    packs, pieces = refs[:-X], refs[-X:]
    heads, _, mine = acc_ref.shape
    columns = []
    for h in range(heads):
        sums = [acc_ref[h, :HEAD_DIM, :]]
        totals = [acc_ref[h, HEAD_DIM : HEAD_DIM + 1, :]]
        tops = [m_ref[h, 0:1, :]]
        for pack in packs:
            sums.append(pack[h * HEAD_DIM : (h + 1) * HEAD_DIM, :].astype(F32))
            stats = pack[heads * HEAD_DIM :, :].astype(F32)
            at = 5 * h
            totals.append(stats[at : at + 1] + stats[at + 1 : at + 2])
            tops.append(stats[at + 2 : at + 3] + stats[at + 3 : at + 4] + stats[at + 4 : at + 5])
        top = functools.reduce(jnp.maximum, tops)
        shares = [jnp.exp2(t - top) for t in tops]
        total = sum(t * s for t, s in zip(totals, shares))
        mixed = sum(a * s for a, s in zip(sums, shares))
        columns.append(mixed / total)
    rows = jnp.concatenate(columns, axis=0).T.astype(BF16)
    block = mine // (X * CORE)
    for core in range(CORE):
        for at, piece in enumerate(pieces):
            start = (core * X + at) * block
            piece[core * block : (core + 1) * block, :] = rows[start : start + block]


def out_rows(piece, w_ref, half):
    width = piece.shape[1]
    here = pl.ds(pl.multiple_of(half * width, width), width)
    return jnp.dot(piece[...], w_ref[here, :], preferred_element_type=F32)


def near_kernel(high_ref, piece, w_ref, out_ref):
    out_ref[...] = out_rows(piece, w_ref, high_ref[0])


def far_kernel(high_ref, near_ref, up, down, across, w_ref, w_side_ref, kept_ref, sent_ref):
    total = near_ref[...] + out_rows(across, w_ref, high_ref[2])
    total = total + out_rows(up, w_side_ref, high_ref[0]) + out_rows(down, w_side_ref, high_ref[1])
    half = kept_ref.shape[0]
    kept_ref[...] = total[:half]
    sent_ref[...] = total[half:].astype(BF16)


def finish_kernel(kept_ref, received_ref, bias_ref, out_ref):
    out_ref[...] = (kept_ref[...] + received_ref[...].astype(F32) + bias_ref[...]).astype(BF16)


def body(
    image_tokens, text_tokens, w_query_key, w_value, qkv_bias, w_text, text_bias, w_out, out_bias
):
    block, model_width = image_tokens.shape
    local_width = w_value.shape[1]
    width = local_width // 2
    heads = width // HEAD_DIM
    mine = block * X * CORE
    queries = mine * Y
    text_count = text_tokens.shape[0]
    text_rows = -(-text_count // 128) * 128
    blk, uly = lax.axis_index("blk"), lax.axis_index("uly")
    x_high = blk // (Y * Z)
    x_at, core_at = x_high * 2 + uly // CORE, uly % CORE

    with jax.named_scope("tokens"):
        near = [image_tokens] + [fetch(image_tokens, dx=d) for d in (1, -1, 2)]

    with jax.named_scope("weights"):
        high = x_high.reshape(1).astype(jnp.int32)

        def halves(*parts):
            columns = sum(p.shape[1] for p in parts) // 2
            return call(
                functools.partial(halves_kernel, width),
                shape((model_width, columns), BF16),
                0,
                *parts,
                scalars=(high,),
                name="halves",
            )

        weights = halves(w_query_key.reshape(model_width, 2 * local_width), w_value)

    with jax.named_scope("project"):
        sibling = fetch(image_tokens, dcore=1)
        near, weights = lax.optimization_barrier((near, weights))
        blocks = near + [sibling] + [fetch(block_rows, dcore=1) for block_rows in near[1:]]
        q_own, kv_own = call(
            project_kernel,
            (shape((heads, HEAD_DIM, mine), BF16), shape((heads, 2 * HEAD_DIM, mine), BF16)),
            6 * mine * model_width * width,
            weights,
            qkv_bias,
            *blocks,
            scalars=(high,),
            scratch=[pltpu.VMEM((mine, model_width), BF16), pltpu.VMEM((8, 3 * width), F32)],
            name="project",
        )
    with jax.named_scope("exchange"):
        up = [fetch(kv_own, dz=1)]
        down = [fetch(kv_own, dz=-1)]
        q_parts = [q_own] + [fetch(q_own, dy=d) for d in (1, -1, 2)]
        for _ in range(2):
            up.append(fetch(up[-1], dz=1))
            down.append(fetch(down[-1], dz=-1))
        w_from, up[1] = lax.optimization_barrier((w_out, up[1]))
        w_side = fetch_x_low(w_from)
        far_keys = fetch(up[-1][:, :HEAD_DIM], dz=1)
        far_values = fetch(down[-1][:, HEAD_DIM:], dz=-1)

    def state_shapes(count):
        return (
            shape((heads, HEAD_DIM + ONES, count), F32),
            shape((heads, 8, count), F32),
            shape((8, 128), F32),
        )

    def query_shapes(count):
        return (shape((heads, 2 * HEAD_DIM, count), BF16), shape((heads, 8, 128), F32))

    def costs(rows, columns):
        return 2500 * heads * rows * columns

    with jax.named_scope("attend"):
        acc, m, bound, q2, norm = call(
            functools.partial(first_kernel, 3, 768),
            state_shapes(queries) + query_shapes(queries),
            costs(queries, 3 * mine),
            *q_parts,
            kv_own,
            up[0],
            down[0],
            exps=0,
            name="attend_first",
        )
        for at in (1, 2):
            acc, m, bound = call(
                functools.partial(next_kernel, 2, 768, None),
                state_shapes(queries),
                costs(queries, 2 * mine),
                up[at],
                down[at],
                q2,
                norm,
                acc,
                m,
                bound,
                exps=0,
                aliases={n + 4: n for n in range(3)},
                name="attend_next",
            )
        pack = shape((heads * HEAD_DIM + STATS, mine), BF16)
        acc, m, bound, *packs = call(
            functools.partial(last_kernel, 1536),
            state_shapes(mine) + (pack,) * (Y - 1),
            costs(queries, mine),
            far_keys,
            far_values,
            q2,
            norm,
            acc,
            m,
            bound,
            exps=0,
            scratch=[pltpu.VMEM(s.shape, s.dtype) for s in state_shapes(queries)[:2]],
            name="attend_last",
        )

    with jax.named_scope("text"):
        packs, w_text, q2, acc = lax.optimization_barrier((packs, w_text, q2, acc))
        text_kv = call(
            text_kernel,
            shape((heads, 2 * HEAD_DIM, text_rows), BF16),
            4 * text_rows * model_width * width,
            text_tokens,
            halves(w_text.reshape(model_width, 2 * local_width)),
            text_bias,
            scalars=(high,),
            scratch=[pltpu.VMEM((text_rows, 2 * width), F32), pltpu.VMEM((8, 2 * width), F32)],
            name="text_project",
        )
        acc, m, _ = call(
            functools.partial(next_kernel, 1, mine, text_count),
            state_shapes(mine),
            costs(mine, text_rows),
            text_kv,
            q2,
            norm,
            acc,
            m,
            bound,
            aliases={n + 3: n for n in range(3)},
            name="attend_text",
        )

    with jax.named_scope("combine"):
        returned = [fetch(pack, dy=-d) for pack, d in zip(packs, (1, -1, 2))]
        piece = shape((CORE * block, width), BF16)
        pieces = call(combine_kernel, (piece,) * X, 0, acc, m, *returned, name="combine")

    with jax.named_scope("output"):
        distances = (1, -1, 2)
        received = [fetch(p, dx=-d) for p, d in zip(pieces[1:], distances)]
        flops = 2 * CORE * block * width * model_width
        total = call(
            near_kernel,
            shape((CORE * block, model_width), F32),
            flops,
            pieces[0],
            w_out,
            scalars=(high,),
            name="output_near",
        )
        received, total = lax.optimization_barrier((received, total))
        highs = jnp.stack([lax.rem(x_at - d + X, X) // 2 for d in distances]).astype(jnp.int32)
        kept, sent = call(
            far_kernel,
            (shape((block, model_width), F32), shape((block, model_width), BF16)),
            3 * flops,
            total,
            *received,
            w_out,
            w_side,
            scalars=(highs,),
            name="output_far",
        )
        return call(
            finish_kernel,
            shape((block, model_width), BF16),
            0,
            kept,
            fetch(sent, dcore=1),
            out_bias.reshape(1, -1),
            name="finish",
        )


def solution(mesh):
    in_specs = (
        P(("uly", "blk"), None),
        P(),
        P(None, None, "uly"),
        P(None, "uly"),
        P(None, "uly"),
        P(None, None, "uly"),
        P(None, "uly"),
        P("uly", None),
        P(),
    )
    out_specs = P(("uly", "blk"), None)
    return jax.shard_map(body, mesh=mesh, in_specs=in_specs, out_specs=out_specs, check_vma=False)
```

```python
import functools

import jax
import jax.numpy as jnp
from jax import lax
from jax.experimental import pallas as pl
from jax.experimental.pallas import tpu as pltpu
from jax.sharding import PartitionSpec as P

HEAD_DIM = 64
AXES = ("uly", "blk")
X, CORE, Y, Z = 4, 2, 4, 8
ONES = 16
VMEM_BYTES = 8 << 20
STATS = 16
LOG2_SCALE = 1.4426950408889634 * HEAD_DIM**-0.5
SAFE_SQUARE = 96.0**2
MASKED = -1e30
BF16, F32 = jnp.bfloat16, jnp.float32


def device_id(x, core, y, z):
    return ((x % 2) * CORE + core) * (2 * Y * Z) + (x // 2) * (Y * Z) + y * Z + z


def places():
    return [
        (x, core, y, z) for x in range(X) for core in range(CORE) for y in range(Y) for z in range(Z)
    ]


def fetch(array, dx=0, dcore=0, dy=0, dz=0):
    pairs = [
        (
            device_id((x + dx) % X, (core + dcore) % CORE, (y + dy) % Y, (z + dz) % Z),
            device_id(x, core, y, z),
        )
        for x, core, y, z in places()
    ]
    return lax.ppermute(array, AXES, pairs)


def fetch_x_low(array):
    pairs = [
        (device_id(x, core, y, z), device_id(x ^ 1, core, y, z)) for x, core, y, z in places()
    ]
    return lax.ppermute(array, AXES, pairs)


def call(kernel, out_shape, flops, *operands, exps=0, aliases=None, scratch=(), scalars=(), name=None):
    spec = pl.BlockSpec(memory_space=pltpu.VMEM)
    scalar_spec = pl.BlockSpec(memory_space=pltpu.SMEM)
    moved = sum(a.size * a.dtype.itemsize for a in operands)
    return pl.pallas_call(
        kernel,
        out_shape=out_shape,
        in_specs=[scalar_spec] * len(scalars) + [spec] * len(operands),
        out_specs=jax.tree.map(lambda _: spec, out_shape),
        input_output_aliases=aliases or {},
        scratch_shapes=scratch,
        compiler_params=pltpu.CompilerParams(vmem_limit_bytes=VMEM_BYTES),
        cost_estimate=pl.CostEstimate(flops=flops, bytes_accessed=moved, transcendentals=exps),
        name=name,
    )(*scalars, *operands)


def shape(dims, dtype):
    return jax.ShapeDtypeStruct(dims, dtype)


def halves_kernel(width, high_ref, *refs):
    parts, out_ref = refs[:-1], refs[-1]
    at = 0
    for part in parts:
        for cut in range(0, part.shape[1], 2 * width):
            low, high = part[:, cut : cut + width], part[:, cut + width : cut + 2 * width]
            out_ref[:, at : at + width] = jnp.where(high_ref[0] == 1, high, low)
            at += width


def half_row(high_ref, bias_ref, row_ref):
    width = bias_ref.shape[1] // 2
    for at in range(bias_ref.shape[0]):
        low, high = bias_ref[at : at + 1, :width], bias_ref[at : at + 1, width:]
        row_ref[0:1, at * width : (at + 1) * width] = jnp.where(high_ref[0] == 1, high, low)
    return row_ref[0:1, :]


def project_kernel(high_ref, w_ref, bias_ref, *refs):
    blocks, (q_ref, kv_ref, tokens, row_ref) = refs[:-4], refs[-4:]
    heads = q_ref.shape[0]
    width = heads * HEAD_DIM
    rows = blocks[0].shape[0]
    for at, block in enumerate(blocks):
        tokens[at * rows : (at + 1) * rows, :] = block[...]
    projected = jnp.dot(tokens[...], w_ref[...], preferred_element_type=F32)
    projected = projected + half_row(high_ref, bias_ref, row_ref)
    columns = projected.T.astype(BF16)
    for h in range(heads):
        cut = h * HEAD_DIM
        q_ref[h] = columns[cut : cut + HEAD_DIM]
        kv_ref[h, :HEAD_DIM, :] = columns[width + cut : width + cut + HEAD_DIM]
        kv_ref[h, HEAD_DIM:, :] = columns[2 * width + cut : 2 * width + cut + HEAD_DIM]


def text_kernel(high_ref, text_ref, w_ref, bias_ref, kv_ref, rows_ref, row_ref):
    heads = kv_ref.shape[0]
    width = heads * HEAD_DIM
    count = text_ref.shape[0]
    rows_ref[...] = jnp.zeros_like(rows_ref)
    rows = jnp.dot(text_ref[...], w_ref[...], preferred_element_type=F32)
    rows_ref[:count, :] = rows + half_row(high_ref, bias_ref, row_ref)
    columns = rows_ref[...].T.astype(BF16)
    for h in range(heads):
        cut = h * HEAD_DIM
        kv_ref[h, :HEAD_DIM, :] = columns[cut : cut + HEAD_DIM]
        kv_ref[h, HEAD_DIM:, :] = columns[width + cut : width + cut + HEAD_DIM]


def scale_queries(parts, q2_ref, norm_ref):
    for h in range(q2_ref.shape[0]):
        largest = None
        for at, part in enumerate(parts):
            scaled = part[h].astype(F32) * LOG2_SCALE
            high = scaled.astype(BF16)
            low = (scaled - high.astype(F32)).astype(BF16)
            here = slice(at * part.shape[2], (at + 1) * part.shape[2])
            q2_ref[h, :HEAD_DIM, here] = high
            q2_ref[h, HEAD_DIM:, here] = low
            top = jnp.max(jnp.sum(scaled * scaled, axis=0, keepdims=True), axis=1, keepdims=True)
            largest = top if largest is None else jnp.maximum(largest, top)
        norm_ref[h] = jnp.broadcast_to(largest, norm_ref.shape[1:])


def keys_of(parts, h):
    return jnp.concatenate([k[h, :HEAD_DIM, :] for k, _ in parts], axis=1)


def values_of(parts, h, count):
    values = jnp.concatenate([v[h, -HEAD_DIM:, :] for _, v in parts], axis=1)
    ones = jnp.ones((ONES, values.shape[1]), BF16)
    if count is not None:
        inside = lax.broadcasted_iota(jnp.int32, ones.shape, 1) < count
        ones = jnp.where(inside, 1.0, 0.0).astype(BF16)
    return jnp.concatenate([values, ones], axis=0)


def attend(parts, q2_ref, norm_ref, bound, state_in, acc_ref, m_ref, bound_ref, tile, count=None):
    heads, _, queries = acc_ref.shape
    worst = None
    for h in range(heads):
        keys = keys_of(parts, h).astype(F32)
        top = jnp.max(jnp.sum(keys * keys, axis=0, keepdims=True), axis=1, keepdims=True)
        product = top * norm_ref[h, 0:1, 0:1]
        worst = product if worst is None else jnp.maximum(worst, product)
    if bound is not None:
        worst = jnp.maximum(worst, bound[0:1, 0:1])
    bound_ref[...] = jnp.broadcast_to(worst, bound_ref.shape)
    safe = jnp.max(worst) <= SAFE_SQUARE

    def doubled_keys(h):
        keys = keys_of(parts, h)
        return jnp.concatenate([keys, keys], axis=0).T

    @pl.when(safe)
    def _():
        def one_head(h, carry):
            keys, values = doubled_keys(h), values_of(parts, h, count)
            for at in range(0, queries, tile):
                here = slice(at, at + tile)
                scores = jnp.dot(keys, q2_ref[h, :, here], preferred_element_type=F32)
                weights = jnp.exp2(scores).astype(BF16)
                term = jnp.dot(values, weights, preferred_element_type=F32)
                acc_ref[h, :, here] = term if state_in is None else state_in[0][h, :, here] + term
            return carry

        lax.fori_loop(0, heads, one_head, 0)
        m_ref[...] = jnp.zeros_like(m_ref) if state_in is None else state_in[1][...]

    @pl.when(jnp.logical_not(safe))
    def _():
        step = 128

        def one_head(h, carry):
            keys, values = doubled_keys(h), values_of(parts, h, count)

            def one_tile(at, carry):
                here = pl.ds(pl.multiple_of(at * step, step), step)
                scores = jnp.dot(keys, q2_ref[h, :, here], preferred_element_type=F32)
                if count is not None:
                    inside = lax.broadcasted_iota(jnp.int32, scores.shape, 0) < count
                    scores = jnp.where(inside, scores, MASKED)
                top = jnp.max(scores, axis=0, keepdims=True)
                if state_in is not None:
                    before = state_in[1][h, 0:1, here]
                    top = jnp.maximum(top, before)
                weights = jnp.exp2(scores - top).astype(BF16)
                term = jnp.dot(values, weights, preferred_element_type=F32)
                if state_in is not None:
                    term = term + state_in[0][h, :, here] * jnp.exp2(before - top)
                acc_ref[h, :, here] = term
                m_ref[h, :, here] = jnp.broadcast_to(top, (m_ref.shape[1], step))
                return carry

            return lax.fori_loop(0, queries // step, one_tile, carry)

        lax.fori_loop(0, heads, one_head, 0)


def first_kernel(n_parts, tile, *refs):
    q_refs, kv_refs = refs[:Y], refs[Y : Y + n_parts]
    acc_ref, m_ref, bound_ref, q2_ref, norm_ref = refs[Y + n_parts :]
    scale_queries(q_refs, q2_ref, norm_ref)
    parts = [(r, r) for r in kv_refs]
    attend(parts, q2_ref, norm_ref, None, None, acc_ref, m_ref, bound_ref, tile)


def next_kernel(n_parts, tile, count, *refs):
    kv_refs, refs = refs[:n_parts], refs[n_parts:]
    q2_ref, norm_ref, acc_in, m_in, bound_in, acc_ref, m_ref, bound_ref = refs
    parts = [(r, r) for r in kv_refs]
    state = (acc_in, m_in)
    attend(parts, q2_ref, norm_ref, bound_in, state, acc_ref, m_ref, bound_ref, tile, count)


def in_parts(value, count):
    parts = []
    for _ in range(count):
        parts.append(value.astype(BF16).astype(F32))
        value = value - parts[-1]
    return parts


def last_kernel(tile, k_ref, v_ref, *refs):
    q2_ref, norm_ref, acc_in, m_in, bound_in, own_acc, own_m, bound_ref = refs[:8]
    packs, (acc_ref, m_ref) = refs[8:-2], refs[-2:]
    parts = [(k_ref, v_ref)]
    state = (acc_in, m_in)
    attend(parts, q2_ref, norm_ref, bound_in, state, acc_ref, m_ref, bound_ref, tile)
    heads, _, queries = q2_ref.shape
    mine = queries // Y
    own_acc[...] = acc_ref[:, :, :mine]
    own_m[...] = m_ref[:, :, :mine]
    for at, pack in enumerate(packs):
        here = slice((at + 1) * mine, (at + 2) * mine)
        rows = []
        for h in range(heads):
            pack[h * HEAD_DIM : (h + 1) * HEAD_DIM, :] = acc_ref[h, :HEAD_DIM, here].astype(BF16)
            rows += in_parts(acc_ref[h, HEAD_DIM : HEAD_DIM + 1, here], 2)
            rows += in_parts(m_ref[h, 0:1, here], 3)
        rows.append(jnp.zeros((STATS - len(rows), mine), F32))
        pack[heads * HEAD_DIM :, :] = jnp.concatenate(rows, axis=0).astype(BF16)


def combine_kernel(acc_ref, m_ref, *refs):
    packs, pieces = refs[:-X], refs[-X:]
    heads, _, mine = acc_ref.shape
    columns = []
    for h in range(heads):
        sums = [acc_ref[h, :HEAD_DIM, :]]
        totals = [acc_ref[h, HEAD_DIM : HEAD_DIM + 1, :]]
        tops = [m_ref[h, 0:1, :]]
        for pack in packs:
            sums.append(pack[h * HEAD_DIM : (h + 1) * HEAD_DIM, :].astype(F32))
            stats = pack[heads * HEAD_DIM :, :].astype(F32)
            at = 5 * h
            totals.append(stats[at : at + 1] + stats[at + 1 : at + 2])
            tops.append(stats[at + 2 : at + 3] + stats[at + 3 : at + 4] + stats[at + 4 : at + 5])
        top = functools.reduce(jnp.maximum, tops)
        shares = [jnp.exp2(t - top) for t in tops]
        total = sum(t * s for t, s in zip(totals, shares))
        mixed = sum(a * s for a, s in zip(sums, shares))
        columns.append(mixed / total)
    rows = jnp.concatenate(columns, axis=0).T.astype(BF16)
    block = mine // (X * CORE)
    for core in range(CORE):
        for at, piece in enumerate(pieces):
            start = (core * X + at) * block
            piece[core * block : (core + 1) * block, :] = rows[start : start + block]


def out_rows(piece, w_ref, half):
    width = piece.shape[1]
    here = pl.ds(pl.multiple_of(half * width, width), width)
    return jnp.dot(piece[...], w_ref[here, :], preferred_element_type=F32)


def near_kernel(high_ref, piece, w_ref, out_ref):
    out_ref[...] = out_rows(piece, w_ref, high_ref[0])


def far_kernel(high_ref, near_ref, across, up, down, w_ref, w_side_ref, kept_ref, sent_ref):
    total = near_ref[...] + out_rows(across, w_ref, high_ref[0])
    total = total + out_rows(up, w_side_ref, high_ref[1]) + out_rows(down, w_side_ref, high_ref[2])
    half = kept_ref.shape[0]
    kept_ref[...] = total[:half]
    sent_ref[...] = total[half:].astype(BF16)


def finish_kernel(kept_ref, received_ref, bias_ref, out_ref):
    out_ref[...] = (kept_ref[...] + received_ref[...].astype(F32) + bias_ref[...]).astype(BF16)


def body(
    image_tokens, text_tokens, w_query_key, w_value, qkv_bias, w_text, text_bias, w_out, out_bias
):
    block, model_width = image_tokens.shape
    local_width = w_value.shape[1]
    width = local_width // 2
    heads = width // HEAD_DIM
    mine = block * X * CORE
    queries = mine * Y
    text_count = text_tokens.shape[0]
    text_rows = -(-text_count // 128) * 128
    blk, uly = lax.axis_index("blk"), lax.axis_index("uly")
    x_high = blk // (Y * Z)
    x_at, core_at = x_high * 2 + uly // CORE, uly % CORE

    with jax.named_scope("tokens"):
        near = [image_tokens] + [fetch(image_tokens, dx=d) for d in (1, -1, 2)]

    with jax.named_scope("weights"):
        high = x_high.reshape(1).astype(jnp.int32)

        def halves(*parts):
            columns = sum(p.shape[1] for p in parts) // 2
            return call(
                functools.partial(halves_kernel, width),
                shape((model_width, columns), BF16),
                0,
                *parts,
                scalars=(high,),
                name="halves",
            )

        weights = halves(w_query_key.reshape(model_width, 2 * local_width), w_value)

    with jax.named_scope("project"):
        sibling = fetch(image_tokens, dcore=1)
        near, weights = lax.optimization_barrier((near, weights))
        blocks = near + [sibling] + [fetch(block_rows, dcore=1) for block_rows in near[1:]]
        q_own, kv_own = call(
            project_kernel,
            (shape((heads, HEAD_DIM, mine), BF16), shape((heads, 2 * HEAD_DIM, mine), BF16)),
            6 * mine * model_width * width,
            weights,
            qkv_bias,
            *blocks,
            scalars=(high,),
            scratch=[pltpu.VMEM((mine, model_width), BF16), pltpu.VMEM((8, 3 * width), F32)],
            name="project",
        )
    with jax.named_scope("exchange"):
        up = [fetch(kv_own, dz=1)]
        down = [fetch(kv_own, dz=-1)]
        q_parts = [q_own] + [fetch(q_own, dy=d) for d in (1, -1, 2)]
        for _ in range(2):
            up.append(fetch(up[-1], dz=1))
            down.append(fetch(down[-1], dz=-1))
        w_from, up[1] = lax.optimization_barrier((w_out, up[1]))
        w_side = fetch_x_low(w_from)
        far_keys = fetch(up[-1][:, :HEAD_DIM], dz=1)
        far_values = fetch(down[-1][:, HEAD_DIM:], dz=-1)

    def state_shapes(count):
        return (
            shape((heads, HEAD_DIM + ONES, count), F32),
            shape((heads, 8, count), F32),
            shape((8, 128), F32),
        )

    def query_shapes(count):
        return (shape((heads, 2 * HEAD_DIM, count), BF16), shape((heads, 8, 128), F32))

    def costs(rows, columns):
        return 2500 * heads * rows * columns

    with jax.named_scope("attend"):
        acc, m, bound, q2, norm = call(
            functools.partial(first_kernel, 3, 768),
            state_shapes(queries) + query_shapes(queries),
            costs(queries, 3 * mine),
            *q_parts,
            kv_own,
            up[0],
            down[0],
            exps=0,
            name="attend_first",
        )
        for at in (1, 2):
            acc, m, bound = call(
                functools.partial(next_kernel, 2, 768, None),
                state_shapes(queries),
                costs(queries, 2 * mine),
                up[at],
                down[at],
                q2,
                norm,
                acc,
                m,
                bound,
                exps=0,
                aliases={n + 4: n for n in range(3)},
                name="attend_next",
            )
        pack = shape((heads * HEAD_DIM + STATS, mine), BF16)
        acc, m, bound, *packs = call(
            functools.partial(last_kernel, 1536),
            state_shapes(mine) + (pack,) * (Y - 1),
            costs(queries, mine),
            far_keys,
            far_values,
            q2,
            norm,
            acc,
            m,
            bound,
            exps=0,
            scratch=[pltpu.VMEM(s.shape, s.dtype) for s in state_shapes(queries)[:2]],
            name="attend_last",
        )

    with jax.named_scope("text"):
        packs, w_text, q2, acc = lax.optimization_barrier((packs, w_text, q2, acc))
        text_kv = call(
            text_kernel,
            shape((heads, 2 * HEAD_DIM, text_rows), BF16),
            4 * text_rows * model_width * width,
            text_tokens,
            halves(w_text.reshape(model_width, 2 * local_width)),
            text_bias,
            scalars=(high,),
            scratch=[pltpu.VMEM((text_rows, 2 * width), F32), pltpu.VMEM((8, 2 * width), F32)],
            name="text_project",
        )
        acc, m, _ = call(
            functools.partial(next_kernel, 1, mine, text_count),
            state_shapes(mine),
            costs(mine, text_rows),
            text_kv,
            q2,
            norm,
            acc,
            m,
            bound,
            aliases={n + 3: n for n in range(3)},
            name="attend_text",
        )

    with jax.named_scope("combine"):
        returned = [fetch(pack, dy=-d) for pack, d in zip(packs, (1, -1, 2))]
        piece = shape((CORE * block, width), BF16)
        pieces = call(combine_kernel, (piece,) * X, 0, acc, m, *returned, name="combine")

    with jax.named_scope("output"):
        distances = (2, 1, -1)
        received = [fetch(pieces[at], dx=-d) for at, d in zip((3, 1, 2), distances)]
        flops = 2 * CORE * block * width * model_width
        total = call(
            near_kernel,
            shape((CORE * block, model_width), F32),
            flops,
            pieces[0],
            w_out,
            scalars=(high,),
            name="output_near",
        )
        received, total = lax.optimization_barrier((received, total))
        highs = jnp.stack([lax.rem(x_at - d + X, X) // 2 for d in distances]).astype(jnp.int32)
        kept, sent = call(
            far_kernel,
            (shape((block, model_width), F32), shape((block, model_width), BF16)),
            3 * flops,
            total,
            *received,
            w_out,
            w_side,
            scalars=(highs,),
            name="output_far",
        )
        return call(
            finish_kernel,
            shape((block, model_width), BF16),
            0,
            kept,
            fetch(sent, dcore=1),
            out_bias.reshape(1, -1),
            name="finish",
        )


def solution(mesh):
    in_specs = (
        P(("uly", "blk"), None),
        P(),
        P(None, None, "uly"),
        P(None, "uly"),
        P(None, "uly"),
        P(None, None, "uly"),
        P(None, "uly"),
        P("uly", None),
        P(),
    )
    out_specs = P(("uly", "blk"), None)
    return jax.shard_map(body, mesh=mesh, in_specs=in_specs, out_specs=out_specs, check_vma=False)
```

```python
import functools

import jax
import jax.numpy as jnp
from jax import lax
from jax.experimental import pallas as pl
from jax.experimental.pallas import tpu as pltpu
from jax.sharding import PartitionSpec as P

HEAD_DIM = 64
AXES = ("uly", "blk")
X, CORE, Y, Z = 4, 2, 4, 8
ONES = 16
VMEM_BYTES = 8 << 20
STATS = 16
LOG2_SCALE = 1.4426950408889634 * HEAD_DIM**-0.5
SAFE_SQUARE = 96.0**2
MASKED = -1e30
BF16, F32 = jnp.bfloat16, jnp.float32


def device_id(x, core, y, z):
    return ((x % 2) * CORE + core) * (2 * Y * Z) + (x // 2) * (Y * Z) + y * Z + z


def places():
    return [
        (x, core, y, z) for x in range(X) for core in range(CORE) for y in range(Y) for z in range(Z)
    ]


def fetch(array, dx=0, dcore=0, dy=0, dz=0):
    pairs = [
        (
            device_id((x + dx) % X, (core + dcore) % CORE, (y + dy) % Y, (z + dz) % Z),
            device_id(x, core, y, z),
        )
        for x, core, y, z in places()
    ]
    return lax.ppermute(array, AXES, pairs)


def fetch_x_low(array):
    pairs = [
        (device_id(x, core, y, z), device_id(x ^ 1, core, y, z)) for x, core, y, z in places()
    ]
    return lax.ppermute(array, AXES, pairs)


def call(kernel, out_shape, flops, *operands, exps=0, aliases=None, scratch=(), scalars=(), name=None):
    spec = pl.BlockSpec(memory_space=pltpu.VMEM)
    scalar_spec = pl.BlockSpec(memory_space=pltpu.SMEM)
    moved = sum(a.size * a.dtype.itemsize for a in operands)
    return pl.pallas_call(
        kernel,
        out_shape=out_shape,
        in_specs=[scalar_spec] * len(scalars) + [spec] * len(operands),
        out_specs=jax.tree.map(lambda _: spec, out_shape),
        input_output_aliases=aliases or {},
        scratch_shapes=scratch,
        compiler_params=pltpu.CompilerParams(vmem_limit_bytes=VMEM_BYTES),
        cost_estimate=pl.CostEstimate(flops=flops, bytes_accessed=moved, transcendentals=exps),
        name=name,
    )(*scalars, *operands)


def shape(dims, dtype):
    return jax.ShapeDtypeStruct(dims, dtype)


def halves_kernel(width, high_ref, *refs):
    parts, out_ref = refs[:-1], refs[-1]
    at = 0
    for part in parts:
        for cut in range(0, part.shape[1], 2 * width):
            low, high = part[:, cut : cut + width], part[:, cut + width : cut + 2 * width]
            out_ref[:, at : at + width] = jnp.where(high_ref[0] == 1, high, low)
            at += width


def half_row(high_ref, bias_ref, row_ref):
    width = bias_ref.shape[1] // 2
    for at in range(bias_ref.shape[0]):
        low, high = bias_ref[at : at + 1, :width], bias_ref[at : at + 1, width:]
        row_ref[0:1, at * width : (at + 1) * width] = jnp.where(high_ref[0] == 1, high, low)
    return row_ref[0:1, :]


def project_kernel(high_ref, w_ref, bias_ref, *refs):
    blocks, (q_ref, kv_ref, tokens, row_ref) = refs[:-4], refs[-4:]
    heads = q_ref.shape[0]
    width = heads * HEAD_DIM
    rows = blocks[0].shape[0]
    for at, block in enumerate(blocks):
        tokens[at * rows : (at + 1) * rows, :] = block[...]
    projected = jnp.dot(tokens[...], w_ref[...], preferred_element_type=F32)
    projected = projected + half_row(high_ref, bias_ref, row_ref)
    columns = projected.T.astype(BF16)
    for h in range(heads):
        cut = h * HEAD_DIM
        q_ref[h] = columns[cut : cut + HEAD_DIM]
        kv_ref[h, :HEAD_DIM, :] = columns[width + cut : width + cut + HEAD_DIM]
        kv_ref[h, HEAD_DIM:, :] = columns[2 * width + cut : 2 * width + cut + HEAD_DIM]


def text_kernel(high_ref, text_ref, w_ref, bias_ref, kv_ref, rows_ref, row_ref):
    heads = kv_ref.shape[0]
    width = heads * HEAD_DIM
    count = text_ref.shape[0]
    rows_ref[...] = jnp.zeros_like(rows_ref)
    rows = jnp.dot(text_ref[...], w_ref[...], preferred_element_type=F32)
    rows_ref[:count, :] = rows + half_row(high_ref, bias_ref, row_ref)
    columns = rows_ref[...].T.astype(BF16)
    for h in range(heads):
        cut = h * HEAD_DIM
        kv_ref[h, :HEAD_DIM, :] = columns[cut : cut + HEAD_DIM]
        kv_ref[h, HEAD_DIM:, :] = columns[width + cut : width + cut + HEAD_DIM]


def scale_queries(parts, q2_ref, norm_ref):
    for h in range(q2_ref.shape[0]):
        largest = None
        for at, part in enumerate(parts):
            scaled = part[h].astype(F32) * LOG2_SCALE
            high = scaled.astype(BF16)
            low = (scaled - high.astype(F32)).astype(BF16)
            here = slice(at * part.shape[2], (at + 1) * part.shape[2])
            q2_ref[h, :HEAD_DIM, here] = high
            q2_ref[h, HEAD_DIM:, here] = low
            top = jnp.max(jnp.sum(scaled * scaled, axis=0, keepdims=True), axis=1, keepdims=True)
            largest = top if largest is None else jnp.maximum(largest, top)
        norm_ref[h] = jnp.broadcast_to(largest, norm_ref.shape[1:])


def keys_of(parts, h):
    return jnp.concatenate([k[h, :HEAD_DIM, :] for k, _ in parts], axis=1)


def values_of(parts, h, count):
    values = jnp.concatenate([v[h, -HEAD_DIM:, :] for _, v in parts], axis=1)
    ones = jnp.ones((ONES, values.shape[1]), BF16)
    if count is not None:
        inside = lax.broadcasted_iota(jnp.int32, ones.shape, 1) < count
        ones = jnp.where(inside, 1.0, 0.0).astype(BF16)
    return jnp.concatenate([values, ones], axis=0)


def attend(parts, q2_ref, norm_ref, bound, state_in, acc_ref, m_ref, bound_ref, tile, count=None):
    heads, _, queries = acc_ref.shape
    worst = None
    for h in range(heads):
        keys = keys_of(parts, h).astype(F32)
        top = jnp.max(jnp.sum(keys * keys, axis=0, keepdims=True), axis=1, keepdims=True)
        product = top * norm_ref[h, 0:1, 0:1]
        worst = product if worst is None else jnp.maximum(worst, product)
    if bound is not None:
        worst = jnp.maximum(worst, bound[0:1, 0:1])
    bound_ref[...] = jnp.broadcast_to(worst, bound_ref.shape)
    safe = jnp.max(worst) <= SAFE_SQUARE

    def doubled_keys(h):
        keys = keys_of(parts, h)
        return jnp.concatenate([keys, keys], axis=0).T

    @pl.when(safe)
    def _():
        def one_head(h, carry):
            keys, values = doubled_keys(h), values_of(parts, h, count)
            for at in range(0, queries, tile):
                here = slice(at, at + tile)
                scores = jnp.dot(keys, q2_ref[h, :, here], preferred_element_type=F32)
                weights = jnp.exp2(scores).astype(BF16)
                term = jnp.dot(values, weights, preferred_element_type=F32)
                acc_ref[h, :, here] = term if state_in is None else state_in[0][h, :, here] + term
            return carry

        lax.fori_loop(0, heads, one_head, 0)
        m_ref[...] = jnp.zeros_like(m_ref) if state_in is None else state_in[1][...]

    @pl.when(jnp.logical_not(safe))
    def _():
        step = 128

        def one_head(h, carry):
            keys, values = doubled_keys(h), values_of(parts, h, count)

            def one_tile(at, carry):
                here = pl.ds(pl.multiple_of(at * step, step), step)
                scores = jnp.dot(keys, q2_ref[h, :, here], preferred_element_type=F32)
                if count is not None:
                    inside = lax.broadcasted_iota(jnp.int32, scores.shape, 0) < count
                    scores = jnp.where(inside, scores, MASKED)
                top = jnp.max(scores, axis=0, keepdims=True)
                if state_in is not None:
                    before = state_in[1][h, 0:1, here]
                    top = jnp.maximum(top, before)
                weights = jnp.exp2(scores - top).astype(BF16)
                term = jnp.dot(values, weights, preferred_element_type=F32)
                if state_in is not None:
                    term = term + state_in[0][h, :, here] * jnp.exp2(before - top)
                acc_ref[h, :, here] = term
                m_ref[h, :, here] = jnp.broadcast_to(top, (m_ref.shape[1], step))
                return carry

            return lax.fori_loop(0, queries // step, one_tile, carry)

        lax.fori_loop(0, heads, one_head, 0)


def first_kernel(n_parts, tile, *refs):
    q_refs, kv_refs = refs[:Y], refs[Y : Y + n_parts]
    acc_ref, m_ref, bound_ref, q2_ref, norm_ref = refs[Y + n_parts :]
    scale_queries(q_refs, q2_ref, norm_ref)
    parts = [(r, r) for r in kv_refs]
    attend(parts, q2_ref, norm_ref, None, None, acc_ref, m_ref, bound_ref, tile)


def next_kernel(n_parts, tile, count, *refs):
    kv_refs, refs = refs[:n_parts], refs[n_parts:]
    q2_ref, norm_ref, acc_in, m_in, bound_in, acc_ref, m_ref, bound_ref = refs
    parts = [(r, r) for r in kv_refs]
    state = (acc_in, m_in)
    attend(parts, q2_ref, norm_ref, bound_in, state, acc_ref, m_ref, bound_ref, tile, count)


def in_parts(value, count):
    parts = []
    for _ in range(count):
        parts.append(value.astype(BF16).astype(F32))
        value = value - parts[-1]
    return parts


def last_kernel(tile, k_ref, v_ref, *refs):
    q2_ref, norm_ref, acc_in, m_in, bound_in, own_acc, own_m, bound_ref = refs[:8]
    packs, (acc_ref, m_ref) = refs[8:-2], refs[-2:]
    parts = [(k_ref, v_ref)]
    state = (acc_in, m_in)
    attend(parts, q2_ref, norm_ref, bound_in, state, acc_ref, m_ref, bound_ref, tile)
    heads, _, queries = q2_ref.shape
    mine = queries // Y
    own_acc[...] = acc_ref[:, :, :mine]
    own_m[...] = m_ref[:, :, :mine]
    for at, pack in enumerate(packs):
        here = slice((at + 1) * mine, (at + 2) * mine)
        rows = []
        for h in range(heads):
            pack[h * HEAD_DIM : (h + 1) * HEAD_DIM, :] = acc_ref[h, :HEAD_DIM, here].astype(BF16)
            rows += in_parts(acc_ref[h, HEAD_DIM : HEAD_DIM + 1, here], 2)
            rows += in_parts(m_ref[h, 0:1, here], 3)
        rows.append(jnp.zeros((STATS - len(rows), mine), F32))
        pack[heads * HEAD_DIM :, :] = jnp.concatenate(rows, axis=0).astype(BF16)


def combine_kernel(acc_ref, m_ref, *refs):
    packs, pieces = refs[:-X], refs[-X:]
    heads, _, mine = acc_ref.shape
    columns = []
    for h in range(heads):
        sums = [acc_ref[h, :HEAD_DIM, :]]
        totals = [acc_ref[h, HEAD_DIM : HEAD_DIM + 1, :]]
        tops = [m_ref[h, 0:1, :]]
        for pack in packs:
            sums.append(pack[h * HEAD_DIM : (h + 1) * HEAD_DIM, :].astype(F32))
            stats = pack[heads * HEAD_DIM :, :].astype(F32)
            at = 5 * h
            totals.append(stats[at : at + 1] + stats[at + 1 : at + 2])
            tops.append(stats[at + 2 : at + 3] + stats[at + 3 : at + 4] + stats[at + 4 : at + 5])
        top = functools.reduce(jnp.maximum, tops)
        shares = [jnp.exp2(t - top) for t in tops]
        total = sum(t * s for t, s in zip(totals, shares))
        mixed = sum(a * s for a, s in zip(sums, shares))
        columns.append(mixed / total)
    rows = jnp.concatenate(columns, axis=0).T.astype(BF16)
    block = mine // (X * CORE)
    for core in range(CORE):
        for at, piece in enumerate(pieces):
            start = (core * X + at) * block
            piece[core * block : (core + 1) * block, :] = rows[start : start + block]


def out_rows(piece, w_ref, half):
    width = piece.shape[1]
    here = pl.ds(pl.multiple_of(half * width, width), width)
    return jnp.dot(piece[...], w_ref[here, :], preferred_element_type=F32)


def near_kernel(high_ref, piece, w_ref, out_ref):
    out_ref[...] = out_rows(piece, w_ref, high_ref[0])


def far_kernel(high_ref, near_ref, across, up, down, w_ref, w_side_ref, kept_ref, sent_ref):
    total = near_ref[...] + out_rows(across, w_ref, high_ref[0])
    total = total + out_rows(up, w_side_ref, high_ref[1]) + out_rows(down, w_side_ref, high_ref[2])
    half = kept_ref.shape[0]
    kept_ref[...] = total[:half]
    sent_ref[...] = total[half:].astype(BF16)


def finish_kernel(kept_ref, received_ref, bias_ref, out_ref):
    out_ref[...] = (kept_ref[...] + received_ref[...].astype(F32) + bias_ref[...]).astype(BF16)


def body(
    image_tokens, text_tokens, w_query_key, w_value, qkv_bias, w_text, text_bias, w_out, out_bias
):
    block, model_width = image_tokens.shape
    local_width = w_value.shape[1]
    width = local_width // 2
    heads = width // HEAD_DIM
    mine = block * X * CORE
    queries = mine * Y
    text_count = text_tokens.shape[0]
    text_rows = -(-text_count // 128) * 128
    blk, uly = lax.axis_index("blk"), lax.axis_index("uly")
    x_high = blk // (Y * Z)
    x_at, core_at = x_high * 2 + uly // CORE, uly % CORE

    with jax.named_scope("tokens"):
        near = [image_tokens] + [fetch(image_tokens, dx=d) for d in (1, -1, 2)]

    with jax.named_scope("weights"):
        high = x_high.reshape(1).astype(jnp.int32)

        def halves(*parts):
            columns = sum(p.shape[1] for p in parts) // 2
            return call(
                functools.partial(halves_kernel, width),
                shape((model_width, columns), BF16),
                0,
                *parts,
                scalars=(high,),
                name="halves",
            )

        weights = halves(w_query_key.reshape(model_width, 2 * local_width), w_value)

    with jax.named_scope("project"):
        sibling = fetch(image_tokens, dcore=1)
        near, weights = lax.optimization_barrier((near, weights))
        blocks = near + [sibling] + [fetch(block_rows, dcore=1) for block_rows in near[1:]]
        q_own, kv_own = call(
            project_kernel,
            (shape((heads, HEAD_DIM, mine), BF16), shape((heads, 2 * HEAD_DIM, mine), BF16)),
            6 * mine * model_width * width,
            weights,
            qkv_bias,
            *blocks,
            scalars=(high,),
            scratch=[pltpu.VMEM((mine, model_width), BF16), pltpu.VMEM((8, 3 * width), F32)],
            name="project",
        )
    with jax.named_scope("exchange"):
        up = [fetch(kv_own, dz=1)]
        down = [fetch(kv_own, dz=-1)]
        q_parts = [q_own] + [fetch(q_own, dy=d) for d in (1, -1, 2)]
        for _ in range(2):
            up.append(fetch(up[-1], dz=1))
            down.append(fetch(down[-1], dz=-1))
        far_keys = fetch(up[-1][:, :HEAD_DIM], dz=1)
        far_values = fetch(down[-1][:, HEAD_DIM:], dz=-1)

    def state_shapes(count):
        return (
            shape((heads, HEAD_DIM + ONES, count), F32),
            shape((heads, 8, count), F32),
            shape((8, 128), F32),
        )

    def query_shapes(count):
        return (shape((heads, 2 * HEAD_DIM, count), BF16), shape((heads, 8, 128), F32))

    def costs(rows, columns):
        return 2500 * heads * rows * columns

    with jax.named_scope("attend"):
        acc, m, bound, q2, norm = call(
            functools.partial(first_kernel, 3, 768),
            state_shapes(queries) + query_shapes(queries),
            costs(queries, 3 * mine),
            *q_parts,
            kv_own,
            up[0],
            down[0],
            exps=0,
            name="attend_first",
        )
        for at in (1, 2):
            acc, m, bound = call(
                functools.partial(next_kernel, 2, 768, None),
                state_shapes(queries),
                costs(queries, 2 * mine),
                up[at],
                down[at],
                q2,
                norm,
                acc,
                m,
                bound,
                exps=0,
                aliases={n + 4: n for n in range(3)},
                name="attend_next",
            )
            if at == 1:
                w_from, acc = lax.optimization_barrier((w_out, acc))
                w_side = fetch_x_low(w_from)
        pack = shape((heads * HEAD_DIM + STATS, mine), BF16)
        acc, m, bound, *packs = call(
            functools.partial(last_kernel, 1536),
            state_shapes(mine) + (pack,) * (Y - 1),
            costs(queries, mine),
            far_keys,
            far_values,
            q2,
            norm,
            acc,
            m,
            bound,
            exps=0,
            scratch=[pltpu.VMEM(s.shape, s.dtype) for s in state_shapes(queries)[:2]],
            name="attend_last",
        )

    with jax.named_scope("text"):
        packs, w_text, q2, acc = lax.optimization_barrier((packs, w_text, q2, acc))
        text_kv = call(
            text_kernel,
            shape((heads, 2 * HEAD_DIM, text_rows), BF16),
            4 * text_rows * model_width * width,
            text_tokens,
            halves(w_text.reshape(model_width, 2 * local_width)),
            text_bias,
            scalars=(high,),
            scratch=[pltpu.VMEM((text_rows, 2 * width), F32), pltpu.VMEM((8, 2 * width), F32)],
            name="text_project",
        )
        acc, m, _ = call(
            functools.partial(next_kernel, 1, mine, text_count),
            state_shapes(mine),
            costs(mine, text_rows),
            text_kv,
            q2,
            norm,
            acc,
            m,
            bound,
            aliases={n + 3: n for n in range(3)},
            name="attend_text",
        )

    with jax.named_scope("combine"):
        returned = [fetch(pack, dy=-d) for pack, d in zip(packs, (1, -1, 2))]
        piece = shape((CORE * block, width), BF16)
        pieces = call(combine_kernel, (piece,) * X, 0, acc, m, *returned, name="combine")

    with jax.named_scope("output"):
        distances = (2, 1, -1)
        received = [fetch(pieces[at], dx=-d) for at, d in zip((3, 1, 2), distances)]
        flops = 2 * CORE * block * width * model_width
        total = call(
            near_kernel,
            shape((CORE * block, model_width), F32),
            flops,
            pieces[0],
            w_out,
            scalars=(high,),
            name="output_near",
        )
        received, total = lax.optimization_barrier((received, total))
        highs = jnp.stack([lax.rem(x_at - d + X, X) // 2 for d in distances]).astype(jnp.int32)
        kept, sent = call(
            far_kernel,
            (shape((block, model_width), F32), shape((block, model_width), BF16)),
            3 * flops,
            total,
            *received,
            w_out,
            w_side,
            scalars=(highs,),
            name="output_far",
        )
        return call(
            finish_kernel,
            shape((block, model_width), BF16),
            0,
            kept,
            fetch(sent, dcore=1),
            out_bias.reshape(1, -1),
            name="finish",
        )


def solution(mesh):
    in_specs = (
        P(("uly", "blk"), None),
        P(),
        P(None, None, "uly"),
        P(None, "uly"),
        P(None, "uly"),
        P(None, None, "uly"),
        P(None, "uly"),
        P("uly", None),
        P(),
    )
    out_specs = P(("uly", "blk"), None)
    return jax.shard_map(body, mesh=mesh, in_specs=in_specs, out_specs=out_specs, check_vma=False)
```
